128 devices in a mesh: member: 8 (over x, y_hi), grid: 16 (over y_lo, z, core).
Axes of the slice: x: 4, y: 4 (y_hi: 2, y_lo: 2; y = y_hi * 2 + y_lo), z: 4, core: 2. Of those that a mesh axis runs over, the one named last changes fastest.
Arguments:
- latent_grids: bfloat16 [8, 8192, 1024], P('member', 'grid'), may hold values from -6 to 6
- cycle_points: int32 [64], replicated, may hold values from 1 to 128, 5120 in all
- norm_gain: float32 [1024], replicated, may hold values from 0.1 to 1.9
- w_query: bfloat16 [1024, 1024], replicated, may hold values from -0.1875 to 0.1875
- w_key: bfloat16 [1024, 1024], replicated, may hold values from -0.1875 to 0.1875
- w_value: bfloat16 [1024, 1024], replicated, may hold values from -0.1875 to 0.1875
- w_out: bfloat16 [1024, 1024], replicated, may hold values from -0.1875 to 0.1875
- dec_gain: float32 [1024], replicated, may hold values from 0.1 to 1.9
- w_dec: bfloat16 [100, 1024], replicated, may hold values from -0.1875 to 0.1875
- target: float32 [100, 8192], P(None, 'grid'), may hold values from -6 to 6
Outputs:
- predicted_maps: bfloat16 [8, 100, 8192], P('member', None, 'grid')
- latent_sensitivity: float32 [8, 8192, 1024], P('member', 'grid')
- out_grad: float32 [1024, 1024], P('grid', 'member')
The draws below stay inside these ranges and needn't reach their ends.
Inputs may be any that keep to these rules, and one draw needn't show every extreme that they name: `cycle_points`: every cycle has at least one live point and at most 128; some cycle is full.
All inputs are finite; a program needn't handle non-finite values.
Results may differ from the reference program's by a relative error of at most 0.038.
Values may be sent and summed in bfloat16 or wider, within the bound.
No kernel may reach another device: no remote copies, remote signals or barrier semaphores. Data moves between devices by JAX's collectives and lax.ppermute only.
A program may use at most 256 MiB of HBM per device.

```python
import math
import jax
import jax.numpy as jnp
import numpy as np
from jax import lax

HEAD_DIM = 64
D = 1024
VARS = 100
CYCLE_MAX = 128
CYCLES_DEV = 4
WINDOW = 256
ENS = 8
CYCLES = 64
POINTS = 8192
N_GRID = 16


def with_spikes(result, rng, source, target, parts, factor):
    def block_of(position):
        return (jnp.arange(result.shape[position]) // (result.shape[position] // parts)).reshape((-1,) + (1,) * (result.ndim - 1 - position))

    first = jax.random.permutation(rng, parts)[block_of(target)]
    second = (block_of(target) + parts // 2) % parts
    return jnp.where((block_of(source) == first) | (block_of(source) == second), factor * result, result)


def level_of(rng, shape, split, least, largest):
    level = 1.0
    for position, blocks in split:
        steps = jax.random.uniform(jax.random.fold_in(jax.random.fold_in(rng, 6), position), (blocks,), jnp.float32, least / len(split), largest / len(split))
        level = level * jnp.repeat(jnp.exp(steps), shape[position] // blocks).reshape((-1,) + (1,) * (len(shape) - 1 - position))
    return level


def split_up(amount, total, bound, skew):
    weights = [(1 << 20) // math.isqrt(grade ** skew) + 1 for grade in range(2, amount + 1)]
    surplus, counts = total - bound - (amount - 1), [1] * (amount - 1)
    while surplus > 0:
        candidates = [i for i in range(amount - 1) if counts[i] < bound]
        pool, remaining = sum([weights[i] for i in candidates]), surplus
        for i in candidates:
            addition = min(bound - counts[i], max(1, remaining * weights[i] // pool), surplus)
            counts[i] = counts[i] + addition
            surplus = surplus - addition
    return np.array([bound] + counts)


def uneven_parts(stream_key, number_of, total, limit, slope):
    if number_of == 2:
        one = jax.random.randint(stream_key, (), max(1, total - limit), min(limit, total - 1) + 1)
        return jnp.stack([one, total - one])
    lengths = jnp.asarray(split_up(number_of, total, limit, slope), jnp.int32)
    pairs = (number_of - 1) // 2
    donor, sink = lengths[1:1 + 2 * pairs:2], lengths[2:2 + 2 * pairs:2]
    slack = jnp.minimum(donor - 1, limit - sink)
    passed = jax.random.randint(jax.random.fold_in(stream_key, 1), (pairs,), 0, 1 << 20) % (slack + 1)
    lengths = lengths.at[1:1 + 2 * pairs:2].set(donor - passed).at[2:2 + 2 * pairs:2].set(sink + passed)
    return lengths[jax.random.permutation(jax.random.fold_in(stream_key, 2), number_of)]


def normal_values(own_key, shape, scale, reach, split=(), kind=jnp.bfloat16):
    factor_of = level_of(own_key, shape, split, -0.22, 0.18) if split else 1.0
    result = jax.random.normal(own_key, shape, jnp.float32) * scale * factor_of
    return jnp.minimum(jnp.maximum(result, -reach), reach).astype(kind)


def bell_draw_with(rng, dims, scale, reach, shards, heavy, kind=jnp.bfloat16):
    drawn = scale * jax.random.normal(rng, dims, jnp.float32)
    if shards:
        drawn = drawn * level_of(rng, dims, shards, -0.22, 0.18)
    return jnp.clip(with_spikes(drawn, jax.random.fold_in(rng, 3), *heavy), -reach, reach).astype(kind)


def setup_inputs(seed: int = 0) -> dict:
    arg_keys = jax.random.split(jax.random.key(seed), 11)
    return {
        "latent_grids": bell_draw_with(arg_keys[0], (ENS, POINTS, D), 1.0, 6.0, ((0, 8), (1, 16)), (1, 2, 16, 2.0)),
        "cycle_points": uneven_parts(arg_keys[1], CYCLES, CYCLES * CYCLE_MAX * 5 // 8, CYCLE_MAX, 2).astype(jnp.int32),
        "norm_gain": jnp.clip(1.0 + 0.18 * jax.random.normal(arg_keys[2], (D,), jnp.float32), 0.1, 1.9),
        "w_query": normal_values(arg_keys[3], (D, D), D ** -0.5, 0.1875),
        "w_key": normal_values(arg_keys[4], (D, D), D ** -0.5, 0.1875),
        "w_value": normal_values(arg_keys[5], (D, D), D ** -0.5, 0.1875),
        "w_out": normal_values(arg_keys[6], (D, D), D ** -0.5, 0.1875),
        "dec_gain": jnp.clip(1.0 + 0.18 * jax.random.normal(arg_keys[7], (D,), jnp.float32), 0.1, 1.9),
        "w_dec": normal_values(arg_keys[8], (VARS, D), D ** -0.5, 0.1875),
        "target": normal_values(arg_keys[9], (VARS, POINTS), 1.0, 6.0, ((1, 16),), jnp.float32),
    }


def rms_norm(values, gain):
    return values * lax.rsqrt(lax.optimization_barrier(jnp.mean(values * values, -1, keepdims=True)) + 1e-05) * gain

def head_norm(values):
    shaped = values.reshape(values.shape[0], -1, HEAD_DIM)
    shaped = shaped * lax.rsqrt(lax.optimization_barrier(jnp.mean(shaped * shaped, -1, keepdims=True)) + 1e-06)
    return shaped.reshape(values.shape)

def live_points(positions, cycle_points, total_slots):
    cycle_ids = jnp.floor_divide(positions, CYCLE_MAX)
    slot_ids = positions - cycle_ids * CYCLE_MAX
    table = jnp.arange(cycle_points.shape[0], dtype=jnp.int32)
    cycle_len = lax.optimization_barrier(jnp.sum(jnp.where(cycle_ids[:, None] == table[None, :], cycle_points[None, :], 0), 1))
    return (slot_ids < cycle_len) & (positions >= 0) & (positions < total_slots)

def band_masks(band_index, row_count, window_rows, total_slots, cycle_points):
    query_pos = band_index * row_count + jnp.arange(row_count, dtype=jnp.int32)
    key_pos = band_index * row_count - window_rows + jnp.arange(row_count + 2 * window_rows, dtype=jnp.int32)
    in_window = jnp.abs(query_pos[:, None] - key_pos[None, :]) <= window_rows
    key_live = live_points(key_pos, cycle_points, total_slots)
    return (in_window & key_live[None, :]).astype(jnp.float32)

def attend(query_bf, pair_bf, key_mask):
    row_count, feature_width = query_bf.shape
    extended_count = pair_bf.shape[0]
    groups = feature_width // (4 * HEAD_DIM)
    queries = query_bf.reshape(row_count, groups, 4, HEAD_DIM).transpose(1, 0, 2, 3)
    key_part = pair_bf[:, :feature_width].reshape(extended_count, groups, 4, HEAD_DIM).transpose(1, 0, 2, 3)
    value_part = pair_bf[:, feature_width:].reshape(extended_count, groups, 4, HEAD_DIM).transpose(1, 0, 2, 3)

    def head_block(operands):
        q_blk, k_blk, v_blk = operands
        scores = jnp.einsum('rhd,ehd->hre', q_blk.astype(jnp.float32), k_blk.astype(jnp.float32), precision=lax.Precision.HIGHEST) * HEAD_DIM ** (-0.5)
        weights = jnp.exp(scores) * key_mask[None]
        weights = weights / lax.optimization_barrier(jnp.sum(weights, -1, keepdims=True))
        weights_bf = weights.astype(jnp.bfloat16)
        return jnp.einsum('hre,ehd->rhd', weights_bf.astype(jnp.float32), v_blk.astype(jnp.float32), precision=lax.Precision.HIGHEST)
    blocks = lax.map(head_block, (queries, key_part, value_part))
    return blocks.transpose(1, 0, 2, 3).reshape(row_count, feature_width)

def decode(level, dec_gain, w_dec):
    decoded = rms_norm(level, dec_gain).astype(jnp.bfloat16)
    return jnp.dot(w_dec, decoded.T, preferred_element_type=jnp.float32)

def kernel_slope(diff):
    return diff * lax.rsqrt(diff * diff + 0.01)

def crps_grad(own_fields, whole_ensemble_decoding, truth_part, live_part):
    ensemble = whole_ensemble_decoding.shape[0]
    pair_sum = lax.optimization_barrier(jnp.sum(kernel_slope(own_fields[:, None] - whole_ensemble_decoding[None]), 1))
    return (kernel_slope(own_fields - truth_part[None]) - pair_sum / (ensemble - 1)) * live_part[None, None, :]

def contract_rows(left, right):
    return lax.dot_general(left, right, (((0,), (0,)), ((), ())), preferred_element_type=jnp.float32)

def contract_cols(left, right):
    return lax.dot_general(left, right, (((1,), (1,)), ((), ())), preferred_element_type=jnp.float32)

def reference(latent_grids, cycle_points, norm_gain, w_query, w_key, w_value, w_out, dec_gain, w_dec, target):
    row_count = CYCLES_DEV * CYCLE_MAX
    window_rows = WINDOW
    feature_width = w_query.shape[0]
    total_slots = POINTS
    ext_rows = row_count + 2 * window_rows
    band_ids = jnp.arange(N_GRID, dtype=jnp.int32)

    def project(current):
        normed = rms_norm(current.astype(jnp.float32), norm_gain).astype(jnp.bfloat16)
        query_raw = jnp.dot(normed, w_query, preferred_element_type=jnp.float32)
        key_raw = jnp.dot(normed, w_key, preferred_element_type=jnp.float32)
        value_raw = jnp.dot(normed, w_value, preferred_element_type=jnp.float32)
        query_bf = head_norm(query_raw).astype(jnp.bfloat16)
        pair_bf = jnp.concatenate([head_norm(key_raw).astype(jnp.bfloat16), value_raw.astype(jnp.bfloat16)], 1)
        return (query_raw, key_raw, query_bf, jnp.pad(pair_bf, ((window_rows, window_rows), (0, 0))))

    def band_inputs(band_index, query_bf, pair_pad):
        start = (band_index * row_count).astype(jnp.int32)
        ext_pair = lax.dynamic_slice_in_dim(pair_pad, start, ext_rows, 0)
        band_query = lax.dynamic_slice_in_dim(query_bf, start, row_count, 0)
        key_mask = band_masks(band_index, row_count, window_rows, total_slots, cycle_points)
        return (band_query, ext_pair, key_mask)

    def evaluate_model(current):
        query_raw, key_raw, query_bf, pair_pad = project(current)

        def band_forward(band_index):
            band_query, ext_pair, key_mask = band_inputs(band_index, query_bf, pair_pad)
            return attend(band_query, ext_pair, key_mask).astype(jnp.bfloat16)
        attended = lax.map(band_forward, band_ids).reshape(total_slots, feature_width)
        level = current.astype(jnp.float32) + jnp.dot(attended, w_out, preferred_element_type=jnp.float32)
        return (decode(level, dec_gain, w_dec).astype(jnp.bfloat16), attended)
    predicted_maps, focused_ensemble_latents = lax.map(evaluate_model, latent_grids)
    live_all = live_points(jnp.arange(total_slots, dtype=jnp.int32), cycle_points, total_slots).astype(jnp.float32)
    whole_ensemble_decoding = predicted_maps.astype(jnp.float32)

    def member_gradient(member_index):
        own_fields = lax.dynamic_slice_in_dim(whole_ensemble_decoding, member_index, 1, 0)
        return crps_grad(own_fields, whole_ensemble_decoding, target, live_all)[0]
    field_grads = lax.map(member_gradient, jnp.arange(ENS, dtype=jnp.int32))

    def backward(operands):
        current, attended, field_grad = operands
        query_raw, key_raw, query_bf, pair_pad = project(current)
        level = current.astype(jnp.float32) + jnp.dot(attended, w_out, preferred_element_type=jnp.float32)
        _, decode_back = jax.vjp(lambda level_in: decode(level_in, dec_gain, w_dec), level)
        level_grad = decode_back(field_grad)[0]
        level_grad_b = level_grad.astype(jnp.bfloat16)
        out_term = contract_rows(attended, level_grad_b)
        attended_grad = contract_cols(level_grad_b, w_out).astype(jnp.bfloat16)

        def band_backward(band_index):
            band_query, ext_pair, key_mask = band_inputs(band_index, query_bf, pair_pad)
            start = (band_index * row_count).astype(jnp.int32)
            cotangent = lax.dynamic_slice_in_dim(attended_grad, start, row_count, 0).astype(jnp.float32)
            _, attend_back = jax.vjp(lambda query_in, pair_in: attend(query_in, pair_in, key_mask), band_query, ext_pair)
            return attend_back(cotangent)
        query_pieces, pair_pieces = lax.map(band_backward, band_ids)

        def add_piece(index, total):
            start = (index * row_count).astype(jnp.int32)
            current_rows = lax.dynamic_slice_in_dim(total, start, ext_rows, 0)
            return lax.dynamic_update_slice_in_dim(total, current_rows + pair_pieces[index].astype(jnp.float32), start, 0)
        pair_total = lax.fori_loop(0, N_GRID, add_piece, jnp.zeros((total_slots + 2 * window_rows, 2 * feature_width), jnp.float32))
        pair_grad = pair_total[window_rows:window_rows + total_slots]
        query_grad = query_pieces.reshape(total_slots, feature_width).astype(jnp.float32)
        query_in = jax.vjp(head_norm, query_raw)[1](query_grad)[0].astype(jnp.bfloat16)
        key_source = jax.vjp(head_norm, key_raw)[1](pair_grad[:, :feature_width])[0].astype(jnp.bfloat16)
        value_in = pair_grad[:, feature_width:].astype(jnp.bfloat16)
        normed_grad = contract_cols(query_in, w_query) + contract_cols(key_source, w_key) + contract_cols(value_in, w_value)
        _, norm_back = jax.vjp(lambda state_in: rms_norm(state_in, norm_gain), current.astype(jnp.float32))
        return (level_grad + norm_back(normed_grad)[0], out_term)
    latent_sensitivity, result_pieces = lax.map(backward, (latent_grids, focused_ensemble_latents, field_grads))
    return (predicted_maps, latent_sensitivity, lax.optimization_barrier(jnp.sum(result_pieces, 0)))
```

```python
import jax
import jax.numpy as jnp
from jax import lax
from jax.experimental import pallas as pl
from jax.experimental.pallas import tpu as pltpu
from jax.sharding import PartitionSpec as P

HEAD_DIM = 64
CYCLE_MAX = 128
WINDOW = 256
ROWS = 512
EXT = 1024
WIDTH = 1024
PAIR = 128
PAIRS = 8
LOG2E = 1.4426950408889634
Q_SCALE = LOG2E * HEAD_DIM**-0.5
DEAD = -30000.0
F32 = jnp.float32
BF16 = jnp.bfloat16


def params(**more):
    return pltpu.CompilerParams(vmem_limit_bytes=56 * 1024 * 1024, **more)


def dot(left, right):
    return lax.dot_general(left, right, (((1,), (0,)), ((), ())), preferred_element_type=F32)


def dot_t(left, right):
    return lax.dot_general(left, right, (((1,), (1,)), ((), ())), preferred_element_type=F32)


def lane(shape):
    return lax.broadcasted_iota(jnp.int32, shape, len(shape) - 1)


def head_mean_matrix(width):
    rows = lax.broadcasted_iota(jnp.int32, (width, width), 0) // HEAD_DIM
    cols = lax.broadcasted_iota(jnp.int32, (width, width), 1) // HEAD_DIM
    return jnp.where(rows == cols, 1.0 / HEAD_DIM, 0.0).astype(BF16)


def normed_rows(x_ref, gain_ref):
    x = x_ref[...].astype(F32)
    scale = lax.rsqrt(jnp.mean(x * x, -1, keepdims=True) + 1e-05)
    return (x * scale * gain_ref[...]).astype(BF16)


def qkv_kernel(x_ref, gain_ref, wq_ref, wk_ref, wv_ref, q_ref, k_ref, v_ref, rq_ref, rk_ref, normed):
    @pl.when(pl.program_id(0) == 0)
    def _():
        normed[...] = normed_rows(x_ref, gain_ref)

    means = head_mean_matrix(256)

    def normalised(raw):
        return lax.rsqrt(dot((raw * raw).astype(BF16), means) + 1e-06)

    rows = normed[...]
    raw = dot(rows, wq_ref[...])
    scale = normalised(raw)
    q_ref[...] = (raw * scale * Q_SCALE).astype(BF16)
    rq_ref[...] = scale.astype(BF16)
    raw = dot(rows, wk_ref[...])
    scale = normalised(raw)
    k_ref[...] = (raw * scale).astype(BF16)
    rk_ref[...] = scale.astype(BF16)
    v_ref[...] = dot(rows, wv_ref[...]).astype(BF16)


def kv_kernel(before_ref, after_ref, gain_ref, wk_ref, wv_ref, k_ref, v_ref, normed):
    @pl.when(pl.program_id(0) == 0)
    def _():
        normed[:256] = normed_rows(before_ref, gain_ref)
        normed[256:] = normed_rows(after_ref, gain_ref)

    means = head_mean_matrix(256)
    rows = normed[...]
    raw = dot(rows, wk_ref[...])
    scale = lax.rsqrt(dot((raw * raw).astype(BF16), means) + 1e-06)
    k_ref[...] = (raw * scale).astype(BF16)
    v_ref[...] = dot(rows, wv_ref[...]).astype(BF16)


def project(x, gain, wq, wk, wv):
    whole = pl.BlockSpec((ROWS, WIDTH), lambda c: (0, 0))
    gains = pl.BlockSpec((1, WIDTH), lambda c: (0, 0))
    weight = pl.BlockSpec((WIDTH, 256), lambda c: (0, c))
    out = pl.BlockSpec((ROWS, 256), lambda c: (0, c))
    shape = jax.ShapeDtypeStruct((ROWS, WIDTH), BF16)
    return pl.pallas_call(
        qkv_kernel,
        grid=(4,),
        in_specs=[whole, gains, weight, weight, weight],
        out_specs=[out] * 5,
        out_shape=[shape] * 5,
        scratch_shapes=[pltpu.VMEM((ROWS, WIDTH), BF16)],
        compiler_params=params(),
        name="project_own",
    )(x, gain, wq, wk, wv)


def project_halo(before, after, gain, wk, wv):
    part = pl.BlockSpec((256, WIDTH), lambda c: (0, 0))
    gains = pl.BlockSpec((1, WIDTH), lambda c: (0, 0))
    weight = pl.BlockSpec((WIDTH, 256), lambda c: (0, c))
    out = pl.BlockSpec((ROWS, 256), lambda c: (0, c))
    shape = jax.ShapeDtypeStruct((ROWS, WIDTH), BF16)
    return pl.pallas_call(
        kv_kernel,
        grid=(4,),
        in_specs=[part, part, gains, weight, weight],
        out_specs=[out] * 2,
        out_shape=[shape] * 2,
        scratch_shapes=[pltpu.VMEM((ROWS, WIDTH), BF16)],
        compiler_params=params(),
        name="project_halo",
    )(before, after, gain, wk, wv)


def key_extras(live_ref):
    pieces = []
    lanes = lane((CYCLE_MAX, PAIR))
    slots = lax.broadcasted_iota(jnp.int32, (CYCLE_MAX, PAIR), 0)
    for cycle in range(EXT // CYCLE_MAX):
        bias = jnp.where(slots < live_ref[cycle], 0.0, DEAD)
        pieces.append(jnp.where(lanes == 0, bias, jnp.where(lanes < 3, 1.0, 0.0)).astype(BF16))
    return pieces


def fill_ext(ext, own_ref, halo_ref):
    ext[:256, :PAIR] = halo_ref[:256]
    ext[256:768, :PAIR] = own_ref[...]
    ext[768:, :PAIR] = halo_ref[256:]


def by_head(value, low):
    zero = jnp.zeros_like(value)
    return jnp.concatenate([jnp.where(low, value, zero), jnp.where(low, zero, value)], 0)


def window_masks():
    rows = lax.broadcasted_iota(jnp.int32, (512, 256), 0) & 255
    cols = lax.broadcasted_iota(jnp.int32, (512, 256), 1)
    return cols >= rows, cols <= rows


def forward_kernel(live_ref, q_ref, k_ref, kh_ref, v_ref, vh_ref, att_ref, eq_ref, kx, vx):
    @pl.when(pl.program_id(0) == 0)
    def _():
        for cycle, piece in enumerate(key_extras(live_ref)):
            kx[cycle * CYCLE_MAX : (cycle + 1) * CYCLE_MAX, PAIR:] = piece
        vx[:, PAIR:] = jnp.ones((EXT, PAIR), BF16)

    fill_ext(kx, k_ref, kh_ref)
    fill_ext(vx, v_ref, vh_ref)
    low = lane((256, PAIR)) < HEAD_DIM
    lanes = lane((512, PAIR))
    one = jnp.where(lanes == 0, 1.0, 0.0).astype(BF16)
    first, last = window_masks()
    for block in range(2):
        left = jnp.concatenate([by_head(q_ref[block * 256 : block * 256 + 256], low), one], 1)
        total = None
        for tile in range(3):
            keys = slice((block + tile) * 256, (block + tile + 1) * 256)
            weights = jnp.exp2(dot_t(left, kx[keys]))
            if tile == 0:
                weights = jnp.where(first, weights, 0.0)
            if tile == 2:
                weights = jnp.where(last, weights, 0.0)
            term = dot(weights.astype(BF16), vx[keys])
            total = term if total is None else total + term
        sums = total[:, PAIR:]
        out = total[:, :PAIR] / sums
        att_ref[block * 256 : block * 256 + 256] = jnp.where(low, out[:256], out[256:]).astype(BF16)
        shift = -jnp.log2(sums)
        high = shift.astype(BF16).astype(F32)
        extras = jnp.where(
            lanes == 0, 1.0, jnp.where(lanes == 1, high, jnp.where(lanes == 2, shift - high, 0.0))
        )
        eq_ref[0, block * 512 : block * 512 + 512] = extras.astype(BF16)


def attention_forward(live, q, k, kh, v, vh):
    part = pl.BlockSpec((ROWS, PAIR), lambda h, _: (0, h))
    return pl.pallas_call(
        forward_kernel,
        grid_spec=pltpu.PrefetchScalarGridSpec(
            num_scalar_prefetch=1,
            grid=(PAIRS,),
            in_specs=[part] * 5,
            out_specs=[part, pl.BlockSpec((1, EXT, PAIR), lambda h, _: (h, 0, 0))],
            scratch_shapes=[pltpu.VMEM((EXT, 2 * PAIR), BF16), pltpu.VMEM((EXT, 2 * PAIR), BF16)],
        ),
        out_shape=[
            jax.ShapeDtypeStruct((ROWS, WIDTH), BF16),
            jax.ShapeDtypeStruct((PAIRS, EXT, PAIR), BF16),
        ],
        compiler_params=params(),
        name="attention_forward",
    )(live, q, k, kh, v, vh)


def backward_kernel(
    live_ref, q_ref, k_ref, kh_ref, v_ref, vh_ref, eq_ref, att_ref, da_ref,
    dq_ref, dk_ref, dv_ref, dkh_ref, dvh_ref, kx, vx, dkt, dvt,
):
    @pl.when(pl.program_id(0) == 0)
    def _():
        for cycle, piece in enumerate(key_extras(live_ref)):
            kx[cycle * CYCLE_MAX : (cycle + 1) * CYCLE_MAX, PAIR:] = piece
            vx[cycle * CYCLE_MAX : (cycle + 1) * CYCLE_MAX, PAIR:] = piece

    fill_ext(kx, k_ref, kh_ref)
    fill_ext(vx, v_ref, vh_ref)
    low = lane((256, PAIR)) < HEAD_DIM
    lanes = lane((512, PAIR))
    first, last = window_masks()
    feature = lax.broadcasted_iota(jnp.int32, (PAIR, 2 * PAIR), 0) // HEAD_DIM
    column = lane((PAIR, 2 * PAIR))
    wanted = (feature == column // PAIR) & ((column % PAIR == 1) | (column % PAIR == 2))
    summing = jnp.where(wanted, 1.0, 0.0).astype(BF16)
    for block in range(2):
        rows = slice(block * 256, block * 256 + 256)
        q = q_ref[rows]
        da = da_ref[rows]
        left = jnp.concatenate([by_head(q, low), eq_ref[0, block * 512 : block * 512 + 512]], 1)
        product = (da.astype(F32) * att_ref[rows].astype(F32)).astype(BF16)
        sums = dot(product, summing)
        sums = jnp.concatenate([sums[:, :PAIR], sums[:, PAIR:]], 0)
        high = sums.astype(BF16).astype(F32)
        offsets = jnp.where(lanes == 2, high - sums, -sums).astype(BF16)
        left_d = jnp.concatenate([by_head(da, low), offsets], 1)
        q_t = q.T
        da_t = da.T
        dq = None
        for tile in range(3):
            place = block + tile
            keys = slice(place * 256, (place + 1) * 256)
            weights = jnp.exp2(dot_t(left, kx[keys]))
            if tile == 0:
                weights = jnp.where(first, weights, 0.0)
            if tile == 2:
                weights = jnp.where(last, weights, 0.0)
            slope = (weights * dot_t(left_d, vx[keys])).astype(BF16)
            weights = weights.astype(BF16)
            term = dot(slope, kx[keys, :PAIR])
            dq = term if dq is None else dq + term
            dk_term = jnp.concatenate(
                [dot(q_t[:HEAD_DIM], slope[:256]), dot(q_t[HEAD_DIM:], slope[256:])], 0
            )
            dv_term = jnp.concatenate(
                [dot(da_t[:HEAD_DIM], weights[:256]), dot(da_t[HEAD_DIM:], weights[256:])], 0
            )
            if block == 1 and tile < 2:
                dkt[:, keys] += dk_term
                dvt[:, keys] += dv_term
            else:
                dkt[:, keys] = dk_term
                dvt[:, keys] = dv_term
        dq = dq * HEAD_DIM**-0.5
        dq_ref[rows] = jnp.where(low, dq[:256], dq[256:]).astype(BF16)
    dk = (dkt[...] * (1.0 / LOG2E)).T.astype(BF16)
    dv = dvt[...].T.astype(BF16)
    dk_ref[...] = dk[256:768]
    dv_ref[...] = dv[256:768]
    dkh_ref[:256] = dk[:256]
    dkh_ref[256:] = dk[768:]
    dvh_ref[:256] = dv[:256]
    dvh_ref[256:] = dv[768:]


def attention_backward(live, q, k, kh, v, vh, eq, att, da):
    part = pl.BlockSpec((ROWS, PAIR), lambda h, _: (0, h))
    shape = jax.ShapeDtypeStruct((ROWS, WIDTH), BF16)
    return pl.pallas_call(
        backward_kernel,
        grid_spec=pltpu.PrefetchScalarGridSpec(
            num_scalar_prefetch=1,
            grid=(PAIRS,),
            in_specs=[part] * 5 + [pl.BlockSpec((1, EXT, PAIR), lambda h, _: (h, 0, 0)), part, part],
            out_specs=[part] * 5,
            scratch_shapes=[
                pltpu.VMEM((EXT, 2 * PAIR), BF16),
                pltpu.VMEM((EXT, 2 * PAIR), BF16),
                pltpu.VMEM((PAIR, EXT), F32),
                pltpu.VMEM((PAIR, EXT), F32),
            ],
        ),
        out_shape=[shape] * 5,
        compiler_params=params(),
        name="attention_backward",
    )(live, q, k, kh, v, vh, eq, att, da)


def decode_kernel(x_ref, att_ref, wo_ref, gain_ref, wd_ref, z_ref, r_ref, field_ref):
    level = x_ref[...].astype(F32) + dot(att_ref[...], wo_ref[...])
    scale = lax.rsqrt(jnp.mean(level * level, -1, keepdims=True) + 1e-05)
    z = level * scale
    z_ref[...] = z.astype(BF16)
    r_ref[...] = jnp.broadcast_to(scale, r_ref.shape)
    decoded = (z * gain_ref[...]).astype(BF16)
    field_ref[...] = dot_t(wd_ref[...], decoded).astype(BF16)


def decode(x, att, wo, gain, wd):
    variables = wd.shape[0]
    rows = pl.BlockSpec((256, WIDTH), lambda b: (b, 0))
    return pl.pallas_call(
        decode_kernel,
        grid=(2,),
        in_specs=[
            rows,
            rows,
            pl.BlockSpec((WIDTH, WIDTH), lambda b: (0, 0)),
            pl.BlockSpec((1, WIDTH), lambda b: (0, 0)),
            pl.BlockSpec((variables, WIDTH), lambda b: (0, 0)),
        ],
        out_specs=[
            rows,
            pl.BlockSpec((256, PAIR), lambda b: (b, 0)),
            pl.BlockSpec((variables, 256), lambda b: (0, b)),
        ],
        out_shape=[
            jax.ShapeDtypeStruct((ROWS, WIDTH), BF16),
            jax.ShapeDtypeStruct((ROWS, PAIR), F32),
            jax.ShapeDtypeStruct((variables, ROWS), BF16),
        ],
        compiler_params=params(),
        name="decode",
    )(x, att, wo, gain, wd)


def kernel_slope(diff):
    return diff * lax.rsqrt(diff * diff + 0.01)


def score_kernel(
    live_ref, own_ref, all_ref, target_ref, z_ref, r_ref, gain_ref, wd_ref, wo_ref, att_ref,
    lg_ref, da_ref, term_ref, total,
):
    step = pl.program_id(0)
    own = own_ref[...].astype(F32)
    members = all_ref.shape[0]
    pair_sum = None
    for member in range(members):
        slope = kernel_slope(own - all_ref[member].astype(F32))
        pair_sum = slope if pair_sum is None else pair_sum + slope
    slots = lane((own.shape[0], CYCLE_MAX))
    live = jnp.concatenate(
        [jnp.where(slots < live_ref[2 + 2 * step + c], 1.0, 0.0) for c in range(2)], 1
    )
    grad = (kernel_slope(own - target_ref[...]) - pair_sum * (1.0 / (members - 1))) * live
    back = lax.dot_general(
        grad.astype(BF16), wd_ref[...], (((0,), (0,)), ((), ())), preferred_element_type=F32
    )
    back = back.astype(BF16).astype(F32) * gain_ref[...]
    z = z_ref[...].astype(F32)
    level_grad = r_ref[:, :1] * (back - z * jnp.mean(back * z, -1, keepdims=True))
    lg = level_grad.astype(BF16)
    lg_ref[...] = lg
    da_ref[...] = dot_t(lg, wo_ref[...]).astype(BF16)
    term = lax.dot_general(att_ref[...], lg, (((0,), (0,)), ((), ())), preferred_element_type=F32)

    @pl.when(step == 0)
    def _():
        total[...] = term

    @pl.when(step == 1)
    def _():
        term_ref[...] = (total[...] + term).astype(BF16)


def score(live, own, everyone, target, z, r, gain, wd, wo, att):
    variables = wd.shape[0]
    members = everyone.shape[0]
    rows = pl.BlockSpec((256, WIDTH), lambda b, _: (b, 0))
    whole = pl.BlockSpec((WIDTH, WIDTH), lambda b, _: (0, 0))
    return pl.pallas_call(
        score_kernel,
        grid_spec=pltpu.PrefetchScalarGridSpec(
            num_scalar_prefetch=1,
            grid=(2,),
            in_specs=[
                pl.BlockSpec((variables, 256), lambda b, _: (0, b)),
                pl.BlockSpec((members, variables, 256), lambda b, _: (0, 0, b)),
                pl.BlockSpec((variables, 256), lambda b, _: (0, b)),
                rows,
                pl.BlockSpec((256, PAIR), lambda b, _: (b, 0)),
                pl.BlockSpec((1, WIDTH), lambda b, _: (0, 0)),
                pl.BlockSpec((variables, WIDTH), lambda b, _: (0, 0)),
                whole,
                rows,
            ],
            out_specs=[rows, rows, whole],
            scratch_shapes=[pltpu.VMEM((WIDTH, WIDTH), F32)],
        ),
        out_shape=[
            jax.ShapeDtypeStruct((ROWS, WIDTH), BF16),
            jax.ShapeDtypeStruct((ROWS, WIDTH), BF16),
            jax.ShapeDtypeStruct((WIDTH, WIDTH), BF16),
        ],
        compiler_params=params(),
        name="score",
    )(live, own, everyone, target, z, r, gain, wd, wo, att)


def final_kernel(
    x_ref, gain_ref, q_ref, k_ref, rq_ref, rk_ref, dq_ref, dk_ref, dv_ref,
    kb_ref, ka_ref, vb_ref, va_ref, wq_ref, wk_ref, wv_ref, lg_ref, out_ref, total,
):
    step = pl.program_id(0)
    means = head_mean_matrix(256)

    def norm_back(y, scale, grad):
        mean = dot((y * grad).astype(BF16), means)
        return (scale.astype(F32) * (grad - y * mean)).astype(BF16)

    def gathered(own_ref, before_ref, after_ref):
        own = own_ref[...].astype(F32)
        halo = jnp.concatenate([before_ref[...], after_ref[...]], 0)
        return own + halo.astype(F32)

    q_in = norm_back(q_ref[...].astype(F32) * (1.0 / Q_SCALE), rq_ref[...], dq_ref[...].astype(F32))
    k_in = norm_back(k_ref[...].astype(F32), rk_ref[...], gathered(dk_ref, kb_ref, ka_ref))
    v_in = gathered(dv_ref, vb_ref, va_ref).astype(BF16)
    term = dot_t(q_in, wq_ref[...]) + dot_t(k_in, wk_ref[...]) + dot_t(v_in, wv_ref[...])

    @pl.when(step == 0)
    def _():
        total[...] = term

    @pl.when(step > 0)
    def _():
        total[...] += term

    @pl.when(step == 3)
    def _():
        for block in range(4):
            rows = slice(block * 128, block * 128 + 128)
            x = x_ref[rows].astype(F32)
            scale = lax.rsqrt(jnp.mean(x * x, -1, keepdims=True) + 1e-05)
            grad = total[rows] * gain_ref[...]
            y = x * scale
            back = scale * (grad - y * jnp.mean(grad * y, -1, keepdims=True))
            out_ref[rows] = lg_ref[rows].astype(F32) + back


def finish(x, gain, q, k, rq, rk, dq, dk, dv, kb, ka, vb, va, wq, wk, wv, lg):
    whole = pl.BlockSpec((ROWS, WIDTH), lambda c: (0, 0))
    gains = pl.BlockSpec((1, WIDTH), lambda c: (0, 0))
    weight = pl.BlockSpec((WIDTH, 256), lambda c: (0, c))
    part = pl.BlockSpec((ROWS, 256), lambda c: (0, c))
    half = pl.BlockSpec((256, 256), lambda c: (0, c))
    return pl.pallas_call(
        final_kernel,
        grid=(4,),
        in_specs=[whole, gains] + [part] * 7 + [half] * 4 + [weight] * 3 + [whole],
        out_specs=whole,
        out_shape=jax.ShapeDtypeStruct((ROWS, WIDTH), F32),
        scratch_shapes=[pltpu.VMEM((ROWS, WIDTH), F32)],
        compiler_params=params(),
        name="finish",
    )(x, gain, q, k, rq, rk, dq, dk, dv, kb, ka, vb, va, wq, wk, wv, lg)


def body(
    latent_grids, cycle_points, norm_gain, w_query, w_key, w_value, w_out, dec_gain, w_dec, target
):
    x = latent_grids[0]
    band = lax.axis_index("grid")
    bands = lax.axis_size("grid")
    up = [(i, i + 1) for i in range(bands - 1)]
    down = [(j, i) for i, j in up]
    norm_gain = norm_gain[None]
    dec_gain = dec_gain[None]
    live = lax.dynamic_slice(jnp.pad(cycle_points, (2, 2)), (band * 4,), (8,))

    before = lax.ppermute(x[256:], "grid", up)
    after = lax.ppermute(x[:256], "grid", down)
    q, k, v, rq, rk = project(x, norm_gain, w_query, w_key, w_value)
    kh, vh = project_halo(before, after, norm_gain, w_key, w_value)
    att, eq = attention_forward(live, q, k, kh, v, vh)
    z, r, field = decode(x, att, w_out, dec_gain, w_dec)
    members = lax.axis_size("member")
    everyone = lax.all_to_all(
        jnp.broadcast_to(field[None], (members, *field.shape)), "member", 0, 0, tiled=True
    )
    lg, da, term = score(live, field, everyone, target, z, r, dec_gain, w_dec, w_out, att)
    dq, dk, dv, dkh, dvh = attention_backward(live, q, k, kh, v, vh, eq, att, da)
    kb = lax.ppermute(dkh[256:], "grid", up)
    ka = lax.ppermute(dkh[:256], "grid", down)
    vb = lax.ppermute(dvh[256:], "grid", up)
    va = lax.ppermute(dvh[:256], "grid", down)
    sens = finish(
        x, norm_gain, q, k, rq, rk, dq, dk, dv, kb, ka, vb, va, w_query, w_key, w_value, lg
    )
    blocks = term.reshape(bands, 64, members, 128).transpose(0, 2, 1, 3)
    blocks = blocks.reshape(bands * members, 64, 128)
    pieces = lax.all_to_all(blocks, ("grid", "member"), 0, 0, tiled=True)
    out = jnp.sum(pieces.astype(F32), 0)
    return (field[None], sens[None], out)


def solution(mesh):
    placed = (P("member", "grid", None), P(), P(), P(), P(), P(), P(), P(), P(), P(None, "grid"))
    return jax.shard_map(
        body,
        mesh=mesh,
        in_specs=placed,
        out_specs=(P("member", None, "grid"), P("member", "grid", None), P("grid", "member")),
        check_vma=False,
    )
```

```python
import jax
import jax.numpy as jnp
from jax import lax
from jax.experimental import pallas as pl
from jax.experimental.pallas import tpu as pltpu
from jax.sharding import PartitionSpec as P

HEAD_DIM = 64
CYCLE_MAX = 128
WINDOW = 256
ROWS = 512
EXT = 1024
WIDTH = 1024
PAIR = 128
PAIRS = 8
LOG2E = 1.4426950408889634
Q_SCALE = LOG2E * HEAD_DIM**-0.5
DEAD = -30000.0
F32 = jnp.float32
BF16 = jnp.bfloat16


def params(mib):
    return pltpu.CompilerParams(vmem_limit_bytes=mib * 1024 * 1024)


def dot(left, right):
    return lax.dot_general(left, right, (((1,), (0,)), ((), ())), preferred_element_type=F32)


def dot_t(left, right):
    return lax.dot_general(left, right, (((1,), (1,)), ((), ())), preferred_element_type=F32)


def lane(shape):
    return lax.broadcasted_iota(jnp.int32, shape, len(shape) - 1)


def head_mean_matrix(width):
    rows = lax.broadcasted_iota(jnp.int32, (width, width), 0) // HEAD_DIM
    cols = lax.broadcasted_iota(jnp.int32, (width, width), 1) // HEAD_DIM
    return jnp.where(rows == cols, 1.0 / HEAD_DIM, 0.0).astype(BF16)


def normed_rows(x_ref, gain_ref):
    x = x_ref[...].astype(F32)
    scale = lax.rsqrt(jnp.mean(x * x, -1, keepdims=True) + 1e-05)
    return (x * scale * gain_ref[...]).astype(BF16)


HBM = pl.BlockSpec(memory_space=pl.ANY)
WHOLE = pl.BlockSpec(memory_space=pltpu.VMEM)


def start_all(sources, targets, semaphores):
    copies = [
        pltpu.make_async_copy(source, target, semaphores.at[place])
        for place, (source, target) in enumerate(zip(sources, targets))
    ]
    for copy in copies:
        copy.start()
    return copies


def wait_all(copies):
    for copy in copies:
        copy.wait()


def head_scales(raw, means, epsilon):
    return [
        lax.rsqrt(dot((part * part).astype(BF16), means) + epsilon)
        for part in (raw[:, c : c + 256] for c in range(0, WIDTH, 256))
    ]


def project_kernel(
    x_hbm, gain_ref, wq_hbm, wk_hbm, wv_hbm, q_hbm, k_hbm, v_hbm, rq_hbm, rk_hbm,
    x, wq, wk, wv, q, k, v, rq, rk, in_sems, out_sems,
):
    loads = start_all((x_hbm, wq_hbm, wk_hbm, wv_hbm), (x, wq, wk, wv), in_sems)
    buffers = (q, rq, k, rk, v)
    outs = (q_hbm, rq_hbm, k_hbm, rk_hbm, v_hbm)
    stores = [
        pltpu.make_async_copy(buffer, out, out_sems.at[place])
        for place, (buffer, out) in enumerate(zip(buffers, outs))
    ]
    means = head_mean_matrix(256)
    loads[0].wait()
    rows = normed_rows(x, gain_ref)
    for weight, out, scale_out, factor, place in ((wq, q, rq, Q_SCALE, 0), (wk, k, rk, 1.0, 1)):
        loads[place + 1].wait()
        raw = dot(rows, weight[...])
        for index, scale in enumerate(head_scales(raw, means, 1e-06)):
            columns = slice(index * 256, index * 256 + 256)
            out[:, columns] = (raw[:, columns] * scale * factor).astype(BF16)
            scale_out[:, columns] = scale.astype(BF16)
        stores[2 * place].start()
        stores[2 * place + 1].start()
    loads[3].wait()
    v[...] = dot(rows, wv[...]).astype(BF16)
    stores[4].start()
    wait_all(stores)


def project(x, gain, wq, wk, wv):
    shape = jax.ShapeDtypeStruct((ROWS, WIDTH), BF16)
    square = pltpu.VMEM((WIDTH, WIDTH), BF16)
    rows = pltpu.VMEM((ROWS, WIDTH), BF16)
    return pl.pallas_call(
        project_kernel,
        in_specs=[HBM, WHOLE, HBM, HBM, HBM],
        out_specs=[HBM] * 5,
        out_shape=[shape] * 5,
        scratch_shapes=[
            rows, square, square, square, rows, rows, rows, rows, rows,
            pltpu.SemaphoreType.DMA((4,)),
            pltpu.SemaphoreType.DMA((5,)),
        ],
        compiler_params=params(56),
        name="project_own",
    )(x, gain, wq, wk, wv)


def key_extras(live_ref):
    pieces = []
    lanes = lane((CYCLE_MAX, PAIR))
    slots = lax.broadcasted_iota(jnp.int32, (CYCLE_MAX, PAIR), 0)
    for cycle in range(EXT // CYCLE_MAX):
        bias = jnp.where(slots < live_ref[cycle], 0.0, DEAD)
        pieces.append(jnp.where(lanes == 0, bias, jnp.where(lanes < 3, 1.0, 0.0)).astype(BF16))
    return pieces


def by_head(value, low):
    zero = jnp.zeros_like(value)
    return jnp.concatenate([jnp.where(low, value, zero), jnp.where(low, zero, value)], 0)


def window_mask(shape, query_dim):
    queries = lax.broadcasted_iota(jnp.int32, shape, query_dim) & 255
    keys = lax.broadcasted_iota(jnp.int32, shape, 1 - query_dim)
    return (keys >= queries) & (keys <= queries + 2 * WINDOW)


def attend_pair(q, kx, vx, low, inside, one):
    lanes = lane((512, PAIR))
    spans = [slice(block * 256, block * 256 + 768) for block in range(2)]
    scores = []
    for block in range(2):
        left = jnp.concatenate([by_head(q[block * 256 : block * 256 + 256], low), one], 1)
        scores.append(dot_t(left, kx[spans[block]]))
    weights = [jnp.where(inside, jnp.exp2(score), 0.0).astype(BF16) for score in scores]
    rows, extras = [], []
    for block in range(2):
        total = dot(weights[block], vx[spans[block]])
        sums = total[:, PAIR:]
        out = total[:, :PAIR] / sums
        rows.append(jnp.where(low, out[:256], out[256:]).astype(BF16))
        shift = -jnp.log2(sums)
        high = shift.astype(BF16).astype(F32)
        extra = jnp.where(
            lanes == 0, 1.0, jnp.where(lanes == 1, high, jnp.where(lanes == 2, shift - high, 0.0))
        )
        extras.append(extra.astype(BF16))
    return rows, extras


def front_kernel(
    live_ref, before_hbm, after_hbm, wk_hbm, wv_hbm, q_hbm, k_hbm, v_hbm, x_hbm, wo_hbm,
    gain_ref, dec_gain_ref, wd_ref,
    kx_hbm, vx_hbm, att_hbm, eq_hbm, z_hbm, r_hbm, field_hbm, copies_hbm,
    halo, wk, wv, q, ke, ve, x, wo, att, eq, z, r, field, kx, vx, in_sems, out_sems,
):
    own = pl.ds(256, 512)
    loads = start_all(
        (before_hbm, after_hbm, wk_hbm, wv_hbm, q_hbm, k_hbm, v_hbm, wo_hbm, x_hbm),
        (halo.at[pl.ds(0, 256)], halo.at[pl.ds(256, 256)], wk, wv, q, ke.at[own], ve.at[own], wo, x),
        in_sems,
    )
    for cycle, piece in enumerate(key_extras(live_ref)):
        kx[cycle * CYCLE_MAX : (cycle + 1) * CYCLE_MAX, PAIR:] = piece
    vx[:, PAIR:] = jnp.ones((EXT, PAIR), BF16)
    means = head_mean_matrix(256)
    wait_all(loads[:3])
    rows = normed_rows(halo, gain_ref)
    raw = dot(rows, wk[...])
    for index, scale in enumerate(head_scales(raw, means, 1e-06)):
        columns = slice(index * 256, index * 256 + 256)
        part = (raw[:, columns] * scale).astype(BF16)
        ke[:256, columns] = part[:256]
        ke[768:, columns] = part[256:]
    loads[3].wait()
    part = dot(rows, wv[...]).astype(BF16)
    ve[:256] = part[:256]
    ve[768:] = part[256:]
    wait_all(loads[4:7])
    stores = start_all((ke, ve), (kx_hbm, vx_hbm), out_sems)
    low = lane((256, PAIR)) < HEAD_DIM
    one = jnp.where(lane((512, PAIR)) == 0, 1.0, 0.0).astype(BF16)
    inside = window_mask((512, 768), 0)

    def pair_step(pair, carry):
        columns = pl.ds(pl.multiple_of(pair * PAIR, PAIR), PAIR)
        kx[:, :PAIR] = ke[:, columns]
        vx[:, :PAIR] = ve[:, columns]
        rows, extras = attend_pair(q[:, columns], kx, vx, low, inside, one)
        for block in range(2):
            att[block * 256 : block * 256 + 256, columns] = rows[block]
            eq[pair, block * 512 : block * 512 + 512] = extras[block]
        return carry

    lax.fori_loop(0, PAIRS, pair_step, 0)
    stores += [
        pltpu.make_async_copy(source, target, out_sems.at[2 + place])
        for place, (source, target) in enumerate(
            ((att, att_hbm), (eq, eq_hbm), (z, z_hbm), (r, r_hbm), (field, field_hbm))
        )
    ]
    stores += [
        pltpu.make_async_copy(field, copies_hbm.at[member], out_sems.at[7 + member])
        for member in range(copies_hbm.shape[0])
    ]
    stores[2].start()
    stores[3].start()
    wait_all(loads[7:])
    level = x[...].astype(F32) + dot(att[...], wo[...])
    scale = lax.rsqrt(jnp.mean(level * level, -1, keepdims=True) + 1e-05)
    normal = level * scale
    decoded = (normal * dec_gain_ref[...]).astype(BF16)
    field[...] = dot_t(wd_ref[...], decoded).astype(BF16)
    for store in stores[6:]:
        store.start()
    z[...] = normal.astype(BF16)
    r[...] = jnp.broadcast_to(scale, r.shape)
    stores[4].start()
    stores[5].start()
    wait_all(stores)


def front(live, before, after, wk, wv, q, k, v, x, wo, gain, dec_gain, wd, members):
    variables = wd.shape[0]
    square = pltpu.VMEM((WIDTH, WIDTH), BF16)
    rows = pltpu.VMEM((ROWS, WIDTH), BF16)
    shape = jax.ShapeDtypeStruct((ROWS, WIDTH), BF16)
    ext = jax.ShapeDtypeStruct((EXT, WIDTH), BF16)
    return pl.pallas_call(
        front_kernel,
        in_specs=[pl.BlockSpec(memory_space=pltpu.SMEM)] + [HBM] * 9 + [WHOLE] * 3,
        out_specs=[HBM] * 8,
        out_shape=[
            ext,
            ext,
            shape,
            jax.ShapeDtypeStruct((PAIRS, EXT, PAIR), BF16),
            shape,
            jax.ShapeDtypeStruct((ROWS, PAIR), F32),
            jax.ShapeDtypeStruct((variables, ROWS), BF16),
            jax.ShapeDtypeStruct((members, variables, ROWS), BF16),
        ],
        scratch_shapes=[
            rows, square, square, rows,
            pltpu.VMEM((EXT, WIDTH), BF16),
            pltpu.VMEM((EXT, WIDTH), BF16),
            rows, square, rows,
            pltpu.VMEM((PAIRS, EXT, PAIR), BF16),
            rows,
            pltpu.VMEM((ROWS, PAIR), F32),
            pltpu.VMEM((variables, ROWS), BF16),
            pltpu.VMEM((EXT, 2 * PAIR), BF16),
            pltpu.VMEM((EXT, 2 * PAIR), BF16),
            pltpu.SemaphoreType.DMA((9,)),
            pltpu.SemaphoreType.DMA((7 + members,)),
        ],
        compiler_params=params(56),
        name="halo_attention_decode",
    )(live, before, after, wk, wv, q, k, v, x, wo, gain, dec_gain, wd)


def backward_kernel(
    live_ref, q_ref, ke_ref, ve_ref, eq_ref, att_ref, da_ref,
    dq_ref, dk_ref, dv_ref, low_ref, high_ref, kx, vx, dka, dva,
):
    @pl.when(pl.program_id(0) == 0)
    def _():
        for cycle, piece in enumerate(key_extras(live_ref)):
            kx[cycle * CYCLE_MAX : (cycle + 1) * CYCLE_MAX, PAIR:] = piece
            vx[cycle * CYCLE_MAX : (cycle + 1) * CYCLE_MAX, PAIR:] = piece

    kx[:, :PAIR] = ke_ref[...]
    vx[:, :PAIR] = ve_ref[...]
    low = lane((256, PAIR)) < HEAD_DIM
    lanes = lane((512, PAIR))
    inside = window_mask((768, 512), 1)
    feature = lax.broadcasted_iota(jnp.int32, (PAIR, 2 * PAIR), 0) // HEAD_DIM
    column = lane((PAIR, 2 * PAIR))
    wanted = (feature == column // PAIR) & ((column % PAIR == 1) | (column % PAIR == 2))
    summing = jnp.where(wanted, 1.0, 0.0).astype(BF16)
    for block in range(2):
        rows = slice(block * 256, block * 256 + 256)
        keys = slice(block * 256, block * 256 + 768)
        q = by_head(q_ref[rows], low)
        da = by_head(da_ref[rows], low)
        left = jnp.concatenate([q, eq_ref[0, block * 512 : block * 512 + 512]], 1)
        product = (da_ref[rows].astype(F32) * att_ref[rows].astype(F32)).astype(BF16)
        sums = dot(product, summing)
        sums = jnp.concatenate([sums[:, :PAIR], sums[:, PAIR:]], 0)
        top = sums.astype(BF16).astype(F32)
        left_d = jnp.concatenate([da, jnp.where(lanes == 2, top - sums, -sums).astype(BF16)], 1)
        weights = jnp.where(inside, jnp.exp2(dot_t(kx[keys], left)), 0.0)
        slope = (weights * dot_t(vx[keys], left_d)).astype(BF16)
        dv = dot(weights.astype(BF16), da)
        dk = dot(slope, q)
        turned = kx[keys, :PAIR].T
        dq = jnp.concatenate(
            [dot(turned[:HEAD_DIM], slope[:, :256]), dot(turned[HEAD_DIM:], slope[:, 256:])], 0
        )
        dq_ref[rows] = (dq * HEAD_DIM**-0.5).T.astype(BF16)
        if block == 0:
            dka[:768] = dk
            dva[:768] = dv
        else:
            dka[256:768] += dk[:512]
            dka[768:] = dk[512:]
            dva[256:768] += dv[:512]
            dva[768:] = dv[512:]
    dk = (dka[...] * (1.0 / LOG2E)).astype(BF16)
    dv = dva[...].astype(BF16)
    dk_ref[...] = dk[256:768]
    dv_ref[...] = dv[256:768]
    low_ref[0] = dk[:256]
    low_ref[1] = dv[:256]
    high_ref[0] = dk[768:]
    high_ref[1] = dv[768:]


def attention_backward(live, q, ke, ve, eq, att, da):
    part = pl.BlockSpec((ROWS, PAIR), lambda h, _: (0, h))
    ext = pl.BlockSpec((EXT, PAIR), lambda h, _: (0, h))
    edge = pl.BlockSpec((2, 256, PAIR), lambda h, _: (0, 0, h))
    shape = jax.ShapeDtypeStruct((ROWS, WIDTH), BF16)
    return pl.pallas_call(
        backward_kernel,
        grid_spec=pltpu.PrefetchScalarGridSpec(
            num_scalar_prefetch=1,
            grid=(PAIRS,),
            in_specs=[part, ext, ext, pl.BlockSpec((1, EXT, PAIR), lambda h, _: (h, 0, 0)), part, part],
            out_specs=[part] * 3 + [edge] * 2,
            scratch_shapes=[
                pltpu.VMEM((EXT, 2 * PAIR), BF16),
                pltpu.VMEM((EXT, 2 * PAIR), BF16),
                pltpu.VMEM((EXT, PAIR), F32),
                pltpu.VMEM((EXT, PAIR), F32),
            ],
        ),
        out_shape=[shape] * 3 + [jax.ShapeDtypeStruct((2, 256, WIDTH), BF16)] * 2,
        compiler_params=params(56),
        name="attention_backward",
    )(live, q, ke, ve, eq, att, da)


def kernel_slope(diff):
    return diff * lax.rsqrt(diff * diff + 0.01)


def score_kernel(
    live_ref, own_ref, all_hbm, target_ref, z_hbm, r_hbm, gain_ref, wd_ref, wo_hbm, att_hbm,
    lg_hbm, da_hbm, term_hbm,
    everyone, z, r, wo, att, lg, da, term, in_sems, out_sems,
):
    loads = start_all(
        (all_hbm, z_hbm, r_hbm, wo_hbm, att_hbm), (everyone, z, r, wo, att), in_sems
    )
    stores = [
        pltpu.make_async_copy(source, target, out_sems.at[place])
        for place, (source, target) in enumerate(((lg, lg_hbm), (da, da_hbm), (term, term_hbm)))
    ]
    members = everyone.shape[0]
    own = own_ref[...].astype(F32)
    slots = lane((own.shape[0], CYCLE_MAX))
    live = jnp.concatenate(
        [jnp.where(slots < live_ref[2 + cycle], 1.0, 0.0) for cycle in range(ROWS // CYCLE_MAX)], 1
    )
    loads[0].wait()
    pair_sum = None
    for member in range(members):
        slope = kernel_slope(own - everyone[member].astype(F32))
        pair_sum = slope if pair_sum is None else pair_sum + slope
    grad = (kernel_slope(own - target_ref[...]) - pair_sum * (1.0 / (members - 1))) * live
    back = lax.dot_general(
        grad.astype(BF16), wd_ref[...], (((0,), (0,)), ((), ())), preferred_element_type=F32
    )
    back = back.astype(BF16).astype(F32) * gain_ref[...]
    wait_all(loads[1:3])
    normal = z[...].astype(F32)
    level_grad = r[:, :1] * (back - normal * jnp.mean(back * normal, -1, keepdims=True))
    lg[...] = level_grad.astype(BF16)
    stores[0].start()
    loads[4].wait()
    whole = lax.dot_general(
        att[...], lg[...], (((0,), (0,)), ((), ())), preferred_element_type=F32
    ).astype(BF16)
    for row in range(term.shape[0]):
        for column in range(term.shape[1]):
            term[row, column] = whole[row * 64 : row * 64 + 64, column * 128 : column * 128 + 128]
    stores[2].start()
    loads[3].wait()
    da[...] = dot_t(lg[...], wo[...]).astype(BF16)
    stores[1].start()
    wait_all(stores)


def score(live, own, everyone, target, z, r, gain, wd, wo, att):
    square = pltpu.VMEM((WIDTH, WIDTH), BF16)
    rows = pltpu.VMEM((ROWS, WIDTH), BF16)
    shape = jax.ShapeDtypeStruct((ROWS, WIDTH), BF16)
    return pl.pallas_call(
        score_kernel,
        in_specs=[pl.BlockSpec(memory_space=pltpu.SMEM), WHOLE, HBM, WHOLE, HBM, HBM, WHOLE, WHOLE, HBM, HBM],
        out_specs=[HBM] * 3,
        out_shape=[shape, shape, jax.ShapeDtypeStruct((16, 8, 64, 128), BF16)],
        scratch_shapes=[
            pltpu.VMEM(everyone.shape, BF16),
            rows,
            pltpu.VMEM((ROWS, PAIR), F32),
            square, rows, rows, rows,
            pltpu.VMEM((16, 8, 64, 128), BF16),
            pltpu.SemaphoreType.DMA((5,)),
            pltpu.SemaphoreType.DMA((3,)),
        ],
        compiler_params=params(56),
        name="score",
    )(live, own, everyone, target, z, r, gain, wd, wo, att)


def final_kernel(
    x_hbm, gain_ref, q_hbm, rq_hbm, dq_hbm, wq_hbm, dv_hbm, before_hbm, after_hbm, wv_hbm,
    dk_hbm, k_hbm, rk_hbm, wk_hbm, lg_hbm, out_hbm,
    x, q, rq, dq, wq, dv, before, after, wv, dk, k, rk, wk, lg, out, in_sems, out_sems,
):
    loads = start_all(
        (q_hbm, rq_hbm, dq_hbm, wq_hbm, dv_hbm, before_hbm, after_hbm, wv_hbm,
         dk_hbm, k_hbm, rk_hbm, wk_hbm, x_hbm, lg_hbm),
        (q, rq, dq, wq, dv, before, after, wv, dk, k, rk, wk, x, lg),
        in_sems,
    )
    means = head_mean_matrix(256)

    def norm_back(y, scale, grad):
        product = (y * grad).astype(BF16)
        mean = jnp.concatenate(
            [dot(product[:, c : c + 256], means) for c in range(0, WIDTH, 256)], 1
        )
        return (scale.astype(F32) * (grad - y * mean)).astype(BF16)

    def gathered(own, kind):
        halo = jnp.concatenate([before[kind], after[kind]], 0)
        return own[...].astype(F32) + halo.astype(F32)

    wait_all(loads[:3])
    q_in = norm_back(q[...].astype(F32) * (1.0 / Q_SCALE), rq[...], dq[...].astype(F32))
    loads[3].wait()
    total = dot_t(q_in, wq[...])
    wait_all(loads[4:8])
    total += dot_t(gathered(dv, 1).astype(BF16), wv[...])
    wait_all(loads[8:12])
    k_in = norm_back(k[...].astype(F32), rk[...], gathered(dk, 0))
    total += dot_t(k_in, wk[...])
    wait_all(loads[12:])
    stores = []
    for block in range(2):
        rows = slice(block * 256, block * 256 + 256)
        state = x[rows].astype(F32)
        scale = lax.rsqrt(jnp.mean(state * state, -1, keepdims=True) + 1e-05)
        grad = total[rows] * gain_ref[...]
        y = state * scale
        back = scale * (grad - y * jnp.mean(grad * y, -1, keepdims=True))
        out[rows] = lg[rows].astype(F32) + back
        place = pl.ds(block * 256, 256)
        stores.append(pltpu.make_async_copy(out.at[place], out_hbm.at[place], out_sems.at[block]))
        stores[-1].start()
    wait_all(stores)


def finish(x, gain, q, k, rq, rk, dq, dk, dv, before, after, wq, wk, wv, lg):
    square = pltpu.VMEM((WIDTH, WIDTH), BF16)
    rows = pltpu.VMEM((ROWS, WIDTH), BF16)
    edge = pltpu.VMEM((2, 256, WIDTH), BF16)
    return pl.pallas_call(
        final_kernel,
        in_specs=[HBM, WHOLE] + [HBM] * 13,
        out_specs=HBM,
        out_shape=jax.ShapeDtypeStruct((ROWS, WIDTH), F32),
        scratch_shapes=[
            rows, rows, rows, rows, square, rows, edge, edge, square, rows, rows, rows, square, rows,
            pltpu.VMEM((ROWS, WIDTH), F32),
            pltpu.SemaphoreType.DMA((14,)),
            pltpu.SemaphoreType.DMA((2,)),
        ],
        compiler_params=params(56),
        name="finish",
    )(x, gain, q, rq, dq, wq, dv, before, after, wv, dk, k, rk, wk, lg)


def body(
    latent_grids, cycle_points, norm_gain, w_query, w_key, w_value, w_out, dec_gain, w_dec, target
):
    x = latent_grids[0]
    band = lax.axis_index("grid")
    bands = lax.axis_size("grid")
    up = [(i, i + 1) for i in range(bands - 1)]
    down = [(j, i) for i, j in up]
    norm_gain = norm_gain[None]
    dec_gain = dec_gain[None]
    live = lax.dynamic_slice(jnp.pad(cycle_points, (2, 2)), (band * 4,), (8,))

    before = lax.ppermute(x[256:], "grid", up)
    after = lax.ppermute(x[:256], "grid", down)
    q, k, v, rq, rk = project(x, norm_gain, w_query, w_key, w_value)
    members = lax.axis_size("member")
    ke, ve, att, eq, z, r, field, copies = front(
        live, before, after, w_key, w_value, q, k, v, x, w_out, norm_gain, dec_gain, w_dec, members
    )
    everyone = lax.all_to_all(copies, "member", 0, 0, tiled=True)
    lg, da, term = score(live, field, everyone, target, z, r, dec_gain, w_dec, w_out, att)
    dq, dk, dv, low, high = attention_backward(live, q, ke, ve, eq, att, da)
    grad_before = lax.ppermute(high, "grid", up)
    grad_after = lax.ppermute(low, "grid", down)
    sens = finish(
        x, norm_gain, q, k, rq, rk, dq, dk, dv, grad_before, grad_after,
        w_query, w_key, w_value, lg,
    )
    blocks = term.reshape(bands * members, 64, 128)
    pieces = lax.all_to_all(blocks, ("grid", "member"), 0, 0, tiled=True)
    out = jnp.sum(pieces.astype(F32), 0)
    return (field[None], sens[None], out)


def solution(mesh):
    placed = (P("member", "grid", None), P(), P(), P(), P(), P(), P(), P(), P(), P(None, "grid"))
    return jax.shard_map(
        body,
        mesh=mesh,
        in_specs=placed,
        out_specs=(P("member", None, "grid"), P("member", "grid", None), P("grid", "member")),
        check_vma=False,
    )
```

```python
import jax
import jax.numpy as jnp
from jax import lax
from jax.experimental import pallas as pl
from jax.experimental.pallas import tpu as pltpu
from jax.sharding import Mesh, PartitionSpec as P

HEAD_DIM = 64
CYCLE_MAX = 128
WINDOW = 256
ROWS = 512
EXT = 1024
WIDTH = 1024
PAIR = 128
PAIRS = 8
LOG2E = 1.4426950408889634
Q_SCALE = LOG2E * HEAD_DIM**-0.5
DEAD = -30000.0
F32 = jnp.float32
BF16 = jnp.bfloat16


def params(mib):
    return pltpu.CompilerParams(vmem_limit_bytes=mib * 1024 * 1024)


def cost(gigaflops):
    return pl.CostEstimate(flops=int(gigaflops * 1e9), bytes_accessed=4 << 20, transcendentals=0)


def dot(left, right):
    return lax.dot_general(left, right, (((1,), (0,)), ((), ())), preferred_element_type=F32)


def dot_t(left, right):
    return lax.dot_general(left, right, (((1,), (1,)), ((), ())), preferred_element_type=F32)


def lane(shape):
    return lax.broadcasted_iota(jnp.int32, shape, len(shape) - 1)


def head_mean_matrix(width):
    rows = lax.broadcasted_iota(jnp.int32, (width, width), 0) // HEAD_DIM
    cols = lax.broadcasted_iota(jnp.int32, (width, width), 1) // HEAD_DIM
    return jnp.where(rows == cols, 1.0 / HEAD_DIM, 0.0).astype(BF16)


def normed_rows(x_ref, gain_ref):
    x = x_ref[...].astype(F32)
    scale = lax.rsqrt(jnp.mean(x * x, -1, keepdims=True) + 1e-05)
    return (x * scale * gain_ref[...]).astype(BF16)


HBM = pl.BlockSpec(memory_space=pl.ANY)
WHOLE = pl.BlockSpec(memory_space=pltpu.VMEM)


def start_all(sources, targets, semaphores):
    copies = [
        pltpu.make_async_copy(source, target, semaphores.at[place])
        for place, (source, target) in enumerate(zip(sources, targets))
    ]
    for copy in copies:
        copy.start()
    return copies


def wait_all(copies):
    for copy in copies:
        copy.wait()


def head_scales(raw, means, epsilon):
    return [
        lax.rsqrt(dot((part * part).astype(BF16), means) + epsilon)
        for part in (raw[:, c : c + 256] for c in range(0, WIDTH, 256))
    ]


def project_kernel(
    x_hbm, gain_ref, wq_hbm, wk_hbm, wv_hbm, q_hbm, k_hbm, v_hbm, rq_hbm, rk_hbm,
    x, wq, wk, wv, q, k, v, rq, rk, in_sems, out_sems,
):
    loads = start_all((x_hbm, wq_hbm, wk_hbm, wv_hbm), (x, wq, wk, wv), in_sems)
    buffers = (q, rq, k, rk, v)
    outs = (q_hbm, rq_hbm, k_hbm, rk_hbm, v_hbm)
    stores = [
        pltpu.make_async_copy(buffer, out, out_sems.at[place])
        for place, (buffer, out) in enumerate(zip(buffers, outs))
    ]
    means = head_mean_matrix(256)
    loads[0].wait()
    rows = normed_rows(x, gain_ref)
    for weight, out, scale_out, factor, place in ((wq, q, rq, Q_SCALE, 0), (wk, k, rk, 1.0, 1)):
        loads[place + 1].wait()
        raw = dot(rows, weight[...])
        for index, scale in enumerate(head_scales(raw, means, 1e-06)):
            columns = slice(index * 256, index * 256 + 256)
            out[:, columns] = (raw[:, columns] * scale * factor).astype(BF16)
            scale_out[:, columns] = scale.astype(BF16)
        stores[2 * place].start()
        stores[2 * place + 1].start()
    loads[3].wait()
    v[...] = dot(rows, wv[...]).astype(BF16)
    stores[4].start()
    wait_all(stores)


def project(x, gain, wq, wk, wv):
    shape = jax.ShapeDtypeStruct((ROWS, WIDTH), BF16)
    square = pltpu.VMEM((WIDTH, WIDTH), BF16)
    rows = pltpu.VMEM((ROWS, WIDTH), BF16)
    return pl.pallas_call(
        project_kernel,
        in_specs=[HBM, WHOLE, HBM, HBM, HBM],
        out_specs=[HBM] * 5,
        out_shape=[shape] * 5,
        scratch_shapes=[
            rows, square, square, square, rows, rows, rows, rows, rows,
            pltpu.SemaphoreType.DMA((4,)),
            pltpu.SemaphoreType.DMA((5,)),
        ],
        compiler_params=params(56),
        name="project_own",
    )(x, gain, wq, wk, wv)


def live_points(cycle_points_ref, cycle):
    index = lax.axis_index(("chip", "core")) * (ROWS // CYCLE_MAX) - WINDOW // CYCLE_MAX + cycle
    count = cycle_points_ref.shape[0]
    points = cycle_points_ref[jnp.clip(index, 0, count - 1)]
    return jnp.where((index >= 0) & (index < count), points, 0)


def key_extras(points_ref):
    pieces = []
    lanes = lane((CYCLE_MAX, PAIR))
    slots = lax.broadcasted_iota(jnp.int32, (CYCLE_MAX, PAIR), 0)
    for cycle in range(EXT // CYCLE_MAX):
        bias = jnp.where(slots < live_points(points_ref, cycle), 0.0, DEAD)
        pieces.append(jnp.where(lanes == 0, bias, jnp.where(lanes < 3, 1.0, 0.0)).astype(BF16))
    return pieces


def by_head(value, low):
    zero = jnp.zeros_like(value)
    return jnp.concatenate([jnp.where(low, value, zero), jnp.where(low, zero, value)], 0)


def window_mask(shape, query_dim):
    queries = lax.broadcasted_iota(jnp.int32, shape, query_dim) & 255
    keys = lax.broadcasted_iota(jnp.int32, shape, 1 - query_dim)
    return (keys >= queries) & (keys <= queries + 2 * WINDOW)


def attend_pair(q, kx, vx, low, inside, one):
    lanes = lane((512, PAIR))
    spans = [slice(block * 256, block * 256 + 768) for block in range(2)]
    scores = []
    for block in range(2):
        left = jnp.concatenate([by_head(q[block * 256 : block * 256 + 256], low), one], 1)
        scores.append(dot_t(left, kx[spans[block]]))
    weights = [jnp.where(inside, jnp.exp2(score), 0.0).astype(BF16) for score in scores]
    rows, extras = [], []
    for block in range(2):
        total = dot(weights[block], vx[spans[block]])
        sums = total[:, PAIR:]
        out = total[:, :PAIR] / sums
        rows.append(jnp.where(low, out[:256], out[256:]).astype(BF16))
        shift = -jnp.log2(sums)
        high = shift.astype(BF16).astype(F32)
        extra = jnp.where(
            lanes == 0, 1.0, jnp.where(lanes == 1, high, jnp.where(lanes == 2, shift - high, 0.0))
        )
        extras.append(extra.astype(BF16))
    return rows, extras


def front_kernel(
    points_ref, before_hbm, after_hbm, wk_hbm, wv_hbm, q_hbm, k_hbm, v_hbm, x_hbm, wo_hbm,
    gain_ref, dec_gain_ref, wd_ref,
    kx_hbm, vx_hbm, att_hbm, eq_hbm, z_hbm, r_hbm, field_hbm, copies_hbm,
    halo, wk, wv, q, ke, ve, x, wo, att, eq, z, r, field, kx, vx, in_sems, out_sems,
):
    own = pl.ds(256, 512)
    loads = start_all(
        (before_hbm, after_hbm, wk_hbm, wv_hbm, q_hbm, k_hbm, v_hbm, wo_hbm, x_hbm),
        (halo.at[pl.ds(0, 256)], halo.at[pl.ds(256, 256)], wk, wv, q, ke.at[own], ve.at[own], wo, x),
        in_sems,
    )
    for cycle, piece in enumerate(key_extras(points_ref)):
        kx[cycle * CYCLE_MAX : (cycle + 1) * CYCLE_MAX, PAIR:] = piece
    vx[:, PAIR:] = jnp.ones((EXT, PAIR), BF16)
    means = head_mean_matrix(256)
    wait_all(loads[:3])
    rows = normed_rows(halo, gain_ref)
    raw = dot(rows, wk[...])
    for index, scale in enumerate(head_scales(raw, means, 1e-06)):
        columns = slice(index * 256, index * 256 + 256)
        part = (raw[:, columns] * scale).astype(BF16)
        ke[:256, columns] = part[:256]
        ke[768:, columns] = part[256:]
    loads[3].wait()
    part = dot(rows, wv[...]).astype(BF16)
    ve[:256] = part[:256]
    ve[768:] = part[256:]
    wait_all(loads[4:7])
    stores = start_all((ke, ve), (kx_hbm, vx_hbm), out_sems)
    low = lane((256, PAIR)) < HEAD_DIM
    one = jnp.where(lane((512, PAIR)) == 0, 1.0, 0.0).astype(BF16)
    inside = window_mask((512, 768), 0)

    def pair_step(pair, carry):
        columns = pl.ds(pl.multiple_of(pair * PAIR, PAIR), PAIR)
        kx[:, :PAIR] = ke[:, columns]
        vx[:, :PAIR] = ve[:, columns]
        rows, extras = attend_pair(q[:, columns], kx, vx, low, inside, one)
        for block in range(2):
            att[block * 256 : block * 256 + 256, columns] = rows[block]
            eq[pair, block * 512 : block * 512 + 512] = extras[block]
        return carry

    lax.fori_loop(0, PAIRS, pair_step, 0)
    stores += [
        pltpu.make_async_copy(source, target, out_sems.at[2 + place])
        for place, (source, target) in enumerate(
            ((att, att_hbm), (eq, eq_hbm), (z, z_hbm), (r, r_hbm), (field, field_hbm))
        )
    ]
    stores += [
        pltpu.make_async_copy(field, copies_hbm.at[member], out_sems.at[7 + member])
        for member in range(copies_hbm.shape[0])
    ]
    stores[2].start()
    stores[3].start()
    wait_all(loads[7:])
    level = x[...].astype(F32) + dot(att[...], wo[...])
    scale = lax.rsqrt(jnp.mean(level * level, -1, keepdims=True) + 1e-05)
    normal = level * scale
    decoded = (normal * dec_gain_ref[...]).astype(BF16)
    field[...] = dot_t(wd_ref[...], decoded).astype(BF16)
    for store in stores[6:]:
        store.start()
    z[...] = normal.astype(BF16)
    r[...] = jnp.broadcast_to(scale, r.shape)
    stores[4].start()
    stores[5].start()
    wait_all(stores)


def front(live, before, after, wk, wv, q, k, v, x, wo, gain, dec_gain, wd, members):
    variables = wd.shape[0]
    square = pltpu.VMEM((WIDTH, WIDTH), BF16)
    rows = pltpu.VMEM((ROWS, WIDTH), BF16)
    shape = jax.ShapeDtypeStruct((ROWS, WIDTH), BF16)
    ext = jax.ShapeDtypeStruct((EXT, WIDTH), BF16)
    return pl.pallas_call(
        front_kernel,
        in_specs=[pl.BlockSpec(memory_space=pltpu.SMEM)] + [HBM] * 9 + [WHOLE] * 3,
        out_specs=[HBM] * 8,
        out_shape=[
            ext,
            ext,
            shape,
            jax.ShapeDtypeStruct((PAIRS, EXT, PAIR), BF16),
            shape,
            jax.ShapeDtypeStruct((ROWS, PAIR), F32),
            jax.ShapeDtypeStruct((variables, ROWS), BF16),
            jax.ShapeDtypeStruct((members, variables, ROWS), BF16),
        ],
        scratch_shapes=[
            rows, square, square, rows,
            pltpu.VMEM((EXT, WIDTH), BF16),
            pltpu.VMEM((EXT, WIDTH), BF16),
            rows, square, rows,
            pltpu.VMEM((PAIRS, EXT, PAIR), BF16),
            rows,
            pltpu.VMEM((ROWS, PAIR), F32),
            pltpu.VMEM((variables, ROWS), BF16),
            pltpu.VMEM((EXT, 2 * PAIR), BF16),
            pltpu.VMEM((EXT, 2 * PAIR), BF16),
            pltpu.SemaphoreType.DMA((9,)),
            pltpu.SemaphoreType.DMA((7 + members,)),
        ],
        compiler_params=params(56),
        name="halo_attention_decode",
    )(live, before, after, wk, wv, q, k, v, x, wo, gain, dec_gain, wd)


def weights_kernel(points_ref, q_ref, ke_ref, eq_ref, edge_ref, own_ref, kx):
    @pl.when(pl.program_id(0) == 0)
    def _():
        for cycle, piece in enumerate(key_extras(points_ref)):
            kx[cycle * CYCLE_MAX : (cycle + 1) * CYCLE_MAX, PAIR:] = piece

    kx[:, :PAIR] = ke_ref[...]
    low = lane((256, PAIR)) < HEAD_DIM
    inside = window_mask((768, 512), 1)
    for block in range(2):
        q = by_head(q_ref[block * 256 : block * 256 + 256], low)
        left = jnp.concatenate([q, eq_ref[0, block * 512 : block * 512 + 512]], 1)
        scores = dot_t(kx[block * 256 : block * 256 + 768], left)
        weights = jnp.where(inside, jnp.exp2(scores), 0.0).astype(BF16)
        edge_ref[0, block] = weights[:256] if block == 0 else weights[512:]
        own_ref[0, block] = weights[256:] if block == 0 else weights[:512]


def attention_weights(live, q, ke, eq):
    part = pl.BlockSpec((ROWS, PAIR), lambda h, _: (0, h))
    ext = pl.BlockSpec((EXT, PAIR), lambda h, _: (0, h))
    return pl.pallas_call(
        weights_kernel,
        grid_spec=pltpu.PrefetchScalarGridSpec(
            num_scalar_prefetch=1,
            grid=(PAIRS,),
            in_specs=[part, ext, pl.BlockSpec((1, EXT, PAIR), lambda h, _: (h, 0, 0))],
            out_specs=[
                pl.BlockSpec((1, 2, 256, 512), lambda h, _: (h, 0, 0, 0)),
                pl.BlockSpec((1, 2, 512, 512), lambda h, _: (h, 0, 0, 0)),
            ],
            scratch_shapes=[pltpu.VMEM((EXT, 2 * PAIR), BF16)],
        ),
        out_shape=[
            jax.ShapeDtypeStruct((PAIRS, 2, 256, 512), BF16),
            jax.ShapeDtypeStruct((PAIRS, 2, 512, 512), BF16),
        ],
        compiler_params=params(56),
        cost_estimate=cost(8),
        name="attention_weights",
    )(live, q, ke, eq)


def slope_operands(q_rows, att_rows, da_rows, low):
    lanes = lane((512, PAIR))
    feature = lax.broadcasted_iota(jnp.int32, (PAIR, 2 * PAIR), 0) // HEAD_DIM
    column = lane((PAIR, 2 * PAIR))
    wanted = (feature == column // PAIR) & ((column % PAIR == 1) | (column % PAIR == 2))
    summing = jnp.where(wanted, 1.0, 0.0).astype(BF16)
    q = by_head(q_rows, low)
    da = by_head(da_rows, low)
    product = (da_rows.astype(F32) * att_rows.astype(F32)).astype(BF16)
    sums = dot(product, summing)
    sums = jnp.concatenate([sums[:, :PAIR], sums[:, PAIR:]], 0)
    top = sums.astype(BF16).astype(F32)
    offsets = jnp.where(lanes == 2, top - sums, -sums).astype(BF16)
    return q, da, jnp.concatenate([da, offsets], 1)


def ones_extra(count):
    lanes = lane((count, PAIR))
    return jnp.where((lanes == 1) | (lanes == 2), 1.0, 0.0).astype(BF16)


def query_piece(keys, slope):
    turned = keys.T
    piece = jnp.concatenate(
        [dot(turned[:HEAD_DIM], slope[:, :256]), dot(turned[HEAD_DIM:], slope[:, 256:])], 0
    )
    return (piece * HEAD_DIM**-0.5).T


def own_kernel(
    q_ref, ka_ref, kb_ref, va_ref, vb_ref, att_ref, da_ref, w_ref, part_ref, dq_ref, dk_ref, dv_ref
):
    low = lane((256, PAIR)) < HEAD_DIM
    values = jnp.concatenate([va_ref[...], vb_ref[...]], 0)
    values = jnp.concatenate([values, ones_extra(512)], 1)
    keys = jnp.concatenate([ka_ref[...], kb_ref[...]], 0)
    operands, slopes = [], []
    for block in range(2):
        rows = slice(block * 256, block * 256 + 256)
        operands.append(slope_operands(q_ref[rows], att_ref[rows], da_ref[rows], low))
        slope = w_ref[0, block].astype(F32) * dot_t(values, operands[block][2])
        slopes.append(slope.astype(BF16))
    weights = jnp.concatenate([w_ref[0, 0], w_ref[0, 1]], 1)
    dv_ref[...] = dot(weights, jnp.concatenate([operands[0][1], operands[1][1]], 0)).astype(BF16)
    dk = dot(jnp.concatenate(slopes, 1), jnp.concatenate([operands[0][0], operands[1][0]], 0))
    dk_ref[...] = (dk * (1.0 / LOG2E)).astype(BF16)
    for block in range(2):
        rows = slice(block * 256, block * 256 + 256)
        piece = query_piece(keys, slopes[block])
        dq_ref[rows] = (part_ref[rows].astype(F32) + piece).astype(BF16)


def own_backward(q, ke, ve, att, da, weights, dq):
    part = pl.BlockSpec((ROWS, PAIR), lambda h: (0, h))
    second = pl.BlockSpec((256, PAIR), lambda h: (1, h))
    third = pl.BlockSpec((256, PAIR), lambda h: (2, h))
    shape = jax.ShapeDtypeStruct((ROWS, WIDTH), BF16)
    return pl.pallas_call(
        own_kernel,
        grid=(PAIRS,),
        in_specs=[part, second, third, second, third, part, part]
        + [pl.BlockSpec((1, 2, 512, 512), lambda h: (h, 0, 0, 0)), part],
        out_specs=[part] * 3,
        out_shape=[shape] * 3,
        compiler_params=params(56),
        cost_estimate=cost(15),
        name="own_backward",
    )(q, ke, ke, ve, ve, att, da, weights, dq)


def kernel_slope(diff):
    return diff * lax.rsqrt(diff * diff + 0.01)


def score_kernel(
    points_ref, own_ref, all_hbm, target_hbm, z_hbm, r_hbm, gain_ref, wd_ref, wo_hbm, att_hbm,
    q_hbm, ke_hbm, ve_hbm, w_hbm,
    lg_hbm, da_hbm, mine_hbm, theirs_hbm, dq_hbm, low_hbm, high_hbm,
    everyone, target, z, r, wo, att, q, ke, ve, w, lg, da, term, dq, edges,
    in_sems, edge_sems, out_sems,
):
    halves = (pl.ds(0, 256), pl.ds(768, 256))
    loads = start_all(
        [all_hbm, target_hbm, z_hbm, r_hbm, att_hbm, wo_hbm, q_hbm]
        + [ref.at[half] for ref in (ve_hbm, ke_hbm) for half in halves]
        + [w_hbm],
        [everyone, target, z, r, att, wo, q]
        + [ref.at[half] for ref in (ve, ke) for half in range(2)]
        + [w],
        in_sems,
    )
    stores = [
        pltpu.make_async_copy(source, place, out_sems.at[index])
        for index, (source, place) in enumerate(
            (
                (lg, lg_hbm),
                (da, da_hbm),
                (term.at[lax.axis_index("core")], mine_hbm),
                (term.at[1 - lax.axis_index("core")], theirs_hbm),
                (dq, dq_hbm),
            )
        )
    ]
    members = everyone.shape[0]
    own = own_ref[...].astype(F32)
    slots = lane((own.shape[0], CYCLE_MAX))
    live = jnp.concatenate(
        [jnp.where(slots < live_points(points_ref, 2 + cycle), 1.0, 0.0) for cycle in range(ROWS // CYCLE_MAX)], 1
    )
    wait_all(loads[:2])
    pair_sum = None
    for member in range(members):
        slope = kernel_slope(own - everyone[member].astype(F32))
        pair_sum = slope if pair_sum is None else pair_sum + slope
    grad = (kernel_slope(own - target[...]) - pair_sum * (1.0 / (members - 1))) * live
    back = lax.dot_general(
        grad.astype(BF16), wd_ref[...], (((0,), (0,)), ((), ())), preferred_element_type=F32
    )
    back = back.astype(BF16).astype(F32) * gain_ref[...]
    wait_all(loads[2:4])
    normal = z[...].astype(F32)
    level_grad = r[:, :1] * (back - normal * jnp.mean(back * normal, -1, keepdims=True))
    lg[...] = level_grad.astype(BF16)
    stores[0].start()
    wait_all(loads[4:6])
    da[...] = dot_t(lg[...], wo[...]).astype(BF16)
    stores[1].start()
    whole = lax.dot_general(
        att[...], lg[...], (((0,), (0,)), ((), ())), preferred_element_type=F32
    ).astype(BF16)
    for row in range(16):
        for column in range(8):
            for half in range(2):
                first = row * 64 + half * 32
                term[half, row, column] = whole[
                    first : first + 32, column * 128 : column * 128 + 128
                ]
    stores[2].start()
    stores[3].start()
    wait_all(loads[6:])

    low = lane((256, PAIR)) < HEAD_DIM
    ones = ones_extra(256)

    def store(pair, block):
        columns = pl.ds(pl.multiple_of(pair * PAIR, PAIR), PAIR)
        place = (low_hbm, high_hbm)[block]
        return pltpu.make_async_copy(
            edges.at[block, :, :, columns], place.at[:, :, columns], edge_sems.at[block, pair]
        )

    def pair_step(step, carry):
        for pair in (step * 2, step * 2 + 1):
            columns = pl.ds(pl.multiple_of(pair * PAIR, PAIR), PAIR)
            for block in range(2):
                rows = slice(block * 256, block * 256 + 256)
                queries, grads, left = slope_operands(
                    q[rows, columns], att[rows, columns], da[rows, columns], low
                )
                weights = w[pair, block]
                slope = dot_t(jnp.concatenate([ve[block, :, columns], ones], 1), left)
                slope = (weights.astype(F32) * slope).astype(BF16)
                edges[block, 0, :, columns] = (dot(slope, queries) * (1.0 / LOG2E)).astype(BF16)
                edges[block, 1, :, columns] = dot(weights, grads).astype(BF16)
                dq[rows, columns] = query_piece(ke[block, :, columns], slope).astype(BF16)
        for pair in (step * 2, step * 2 + 1):
            for block in range(2):
                store(pair, block).start()
        return carry

    lax.fori_loop(0, PAIRS // 2, pair_step, 0)
    stores[4].start()
    for pair in range(PAIRS):
        for block in range(2):
            store(pair, block).wait()
    wait_all(stores)


def score(live, own, everyone, target, z, r, gain, wd, wo, att, q, ke, ve, weights):
    square = pltpu.VMEM((WIDTH, WIDTH), BF16)
    rows = pltpu.VMEM((ROWS, WIDTH), BF16)
    halves = pltpu.VMEM((2, 256, WIDTH), BF16)
    shape = jax.ShapeDtypeStruct((ROWS, WIDTH), BF16)
    edge = jax.ShapeDtypeStruct((2, 256, WIDTH), BF16)
    term = jax.ShapeDtypeStruct((16, 8, 32, 128), BF16)
    return pl.pallas_call(
        score_kernel,
        in_specs=[pl.BlockSpec(memory_space=pltpu.SMEM), WHOLE]
        + [HBM] * 4 + [WHOLE] * 2 + [HBM] * 6,
        out_specs=[HBM] * 7,
        out_shape=[shape, shape, term, term, shape, edge, edge],
        scratch_shapes=[
            pltpu.VMEM(everyone.shape, BF16),
            pltpu.VMEM(target.shape, F32),
            rows,
            pltpu.VMEM((ROWS, PAIR), F32),
            square, rows, rows, halves, halves,
            pltpu.VMEM((PAIRS, 2, 256, 512), BF16),
            rows, rows,
            pltpu.VMEM((2, 16, 8, 32, 128), BF16),
            rows,
            pltpu.VMEM((2, 2, 256, WIDTH), BF16),
            pltpu.SemaphoreType.DMA((12,)),
            pltpu.SemaphoreType.DMA((2, PAIRS)),
            pltpu.SemaphoreType.DMA((5,)),
        ],
        compiler_params=params(56),
        cost_estimate=cost(15),
        name="score_and_edges",
    )(live, own, everyone, target, z, r, gain, wd, wo, att, q, ke, ve, weights)


def final_kernel(
    x_hbm, gain_ref, q_hbm, rq_hbm, dq_hbm, wq_hbm, dv_hbm, before_hbm, after_hbm, wv_hbm,
    dk_hbm, k_hbm, rk_hbm, wk_hbm, lg_hbm, out_hbm,
    x, q, rq, dq, wq, dv, before, after, wv, dk, k, rk, wk, lg, out, in_sems, out_sems,
):
    loads = start_all(
        (q_hbm, rq_hbm, dq_hbm, wq_hbm, dv_hbm, before_hbm, after_hbm, wv_hbm,
         dk_hbm, k_hbm, rk_hbm, wk_hbm, x_hbm, lg_hbm),
        (q, rq, dq, wq, dv, before, after, wv, dk, k, rk, wk, x, lg),
        in_sems,
    )
    means = head_mean_matrix(256)

    def norm_back(y, scale, grad):
        product = (y * grad).astype(BF16)
        mean = jnp.concatenate(
            [dot(product[:, c : c + 256], means) for c in range(0, WIDTH, 256)], 1
        )
        return (scale.astype(F32) * (grad - y * mean)).astype(BF16)

    def gathered(own, kind):
        halo = jnp.concatenate([before[kind], after[kind]], 0)
        return own[...].astype(F32) + halo.astype(F32)

    wait_all(loads[:3])
    q_in = norm_back(q[...].astype(F32) * (1.0 / Q_SCALE), rq[...], dq[...].astype(F32))
    loads[3].wait()
    total = dot_t(q_in, wq[...])
    wait_all(loads[4:8])
    total += dot_t(gathered(dv, 1).astype(BF16), wv[...])
    wait_all(loads[8:12])
    k_in = norm_back(k[...].astype(F32), rk[...], gathered(dk, 0))
    total += dot_t(k_in, wk[...])
    wait_all(loads[12:])
    stores = []
    for block in range(2):
        rows = slice(block * 256, block * 256 + 256)
        state = x[rows].astype(F32)
        scale = lax.rsqrt(jnp.mean(state * state, -1, keepdims=True) + 1e-05)
        grad = total[rows] * gain_ref[...]
        y = state * scale
        back = scale * (grad - y * jnp.mean(grad * y, -1, keepdims=True))
        out[rows] = lg[rows].astype(F32) + back
        place = pl.ds(block * 256, 256)
        stores.append(pltpu.make_async_copy(out.at[place], out_hbm.at[place], out_sems.at[block]))
        stores[-1].start()
    wait_all(stores)


def finish(x, gain, q, k, rq, rk, dq, dk, dv, before, after, wq, wk, wv, lg):
    square = pltpu.VMEM((WIDTH, WIDTH), BF16)
    rows = pltpu.VMEM((ROWS, WIDTH), BF16)
    edge = pltpu.VMEM((2, 256, WIDTH), BF16)
    return pl.pallas_call(
        final_kernel,
        in_specs=[HBM, WHOLE] + [HBM] * 13,
        out_specs=HBM,
        out_shape=jax.ShapeDtypeStruct((ROWS, WIDTH), F32),
        scratch_shapes=[
            rows, rows, rows, rows, square, rows, edge, edge, square, rows, rows, rows, square, rows,
            pltpu.VMEM((ROWS, WIDTH), F32),
            pltpu.SemaphoreType.DMA((14,)),
            pltpu.SemaphoreType.DMA((2,)),
        ],
        compiler_params=params(56),
        name="finish",
    )(x, gain, q, rq, dq, wq, dv, before, after, wv, dk, k, rk, wk, lg)


def body(
    latent_grids, cycle_points, norm_gain, w_query, w_key, w_value, w_out, dec_gain, w_dec, target
):
    x = latent_grids[0]
    grid = ("chip", "core")
    bands = lax.axis_size(grid)
    up = [(i, i + 1) for i in range(bands - 1)]
    down = [(j, i) for i, j in up]
    norm_gain = norm_gain[None]
    dec_gain = dec_gain[None]

    before = lax.ppermute(x[256:], grid, up)
    after = lax.ppermute(x[:256], grid, down)
    q, k, v, rq, rk = project(x, norm_gain, w_query, w_key, w_value)
    members = lax.axis_size("member")
    ke, ve, att, eq, z, r, field, copies = front(
        cycle_points, before, after, w_key, w_value, q, k, v, x, w_out, norm_gain, dec_gain, w_dec, members
    )
    everyone = lax.all_to_all(copies, "member", 0, 0, tiled=True)
    edge_weights, own_weights = attention_weights(cycle_points, q, ke, eq)
    lg, da, mine, theirs, dq, low, high = score(
        cycle_points, field, everyone, target, z, r, dec_gain, w_dec, w_out, att, q, ke, ve, edge_weights
    )
    sibling = lax.ppermute(theirs, "core", [(0, 1), (1, 0)])
    grad_before = lax.ppermute(high, grid, up)
    grad_after = lax.ppermute(low, grid, down)
    dq, dk, dv = own_backward(q, ke, ve, att, da, own_weights, dq)
    sens = finish(
        x, norm_gain, q, k, rq, rk, dq, dk, dv, grad_before, grad_after,
        w_query, w_key, w_value, lg,
    )
    blocks = (mine.astype(F32) + sibling.astype(F32)).astype(BF16)
    pieces = lax.all_to_all(
        blocks.reshape(128, 32, 128), ("chip", "core", "member"), 0, 0, tiled=True
    )
    halves = jnp.sum(pieces.reshape(8, 2, 8, 32, 128).astype(F32), (0, 2))
    out = halves.reshape(64, 128)
    return (field[None], sens[None], out)


def solution(mesh):
    members, bands = mesh.devices.shape
    mesh = Mesh(mesh.devices.reshape(members, bands // 2, 2), ("member", "chip", "core"))
    grid = ("chip", "core")
    placed = (P("member", grid, None), P(), P(), P(), P(), P(), P(), P(), P(), P(None, grid))
    return jax.shard_map(
        body,
        mesh=mesh,
        in_specs=placed,
        out_specs=(P("member", None, grid), P("member", grid, None), P(grid, "member")),
        check_vma=False,
    )
```

```python
import jax
import jax.numpy as jnp
from jax import lax
from jax.experimental import pallas as pl
from jax.experimental.pallas import tpu as pltpu
from jax.sharding import Mesh, PartitionSpec as P

HEAD_DIM = 64
CYCLE_MAX = 128
WINDOW = 256
ROWS = 512
EXT = 1024
WIDTH = 1024
PAIR = 128
PAIRS = 8
LOG2E = 1.4426950408889634
Q_SCALE = LOG2E * HEAD_DIM**-0.5
DEAD = -30000.0
F32 = jnp.float32
BF16 = jnp.bfloat16


def params(mib):
    return pltpu.CompilerParams(vmem_limit_bytes=mib * 1024 * 1024)


def cost(gigaflops):
    return pl.CostEstimate(flops=int(gigaflops * 1e9), bytes_accessed=4 << 20, transcendentals=0)


def dot(left, right):
    return lax.dot_general(left, right, (((1,), (0,)), ((), ())), preferred_element_type=F32)


def dot_t(left, right):
    return lax.dot_general(left, right, (((1,), (1,)), ((), ())), preferred_element_type=F32)


def lane(shape):
    return lax.broadcasted_iota(jnp.int32, shape, len(shape) - 1)


def head_mean_matrix(width):
    rows = lax.broadcasted_iota(jnp.int32, (width, width), 0) // HEAD_DIM
    cols = lax.broadcasted_iota(jnp.int32, (width, width), 1) // HEAD_DIM
    return jnp.where(rows == cols, 1.0 / HEAD_DIM, 0.0).astype(BF16)


def normed_rows(x_ref, gain_ref):
    x = x_ref[...].astype(F32)
    scale = lax.rsqrt(jnp.mean(x * x, -1, keepdims=True) + 1e-05)
    return (x * scale * gain_ref[...]).astype(BF16)


HBM = pl.BlockSpec(memory_space=pl.ANY)
WHOLE = pl.BlockSpec(memory_space=pltpu.VMEM)


def start_all(sources, targets, semaphores):
    copies = [
        pltpu.make_async_copy(source, target, semaphores.at[place])
        for place, (source, target) in enumerate(zip(sources, targets))
    ]
    for copy in copies:
        copy.start()
    return copies


def wait_all(copies):
    for copy in copies:
        copy.wait()


def head_scales(raw, means, epsilon):
    return [
        lax.rsqrt(dot((part * part).astype(BF16), means) + epsilon)
        for part in (raw[:, c : c + 256] for c in range(0, WIDTH, 256))
    ]


def project_kernel(
    x_hbm, gain_ref, wq_hbm, wk_hbm, wv_hbm, q_hbm, k_hbm, v_hbm, rq_hbm, rk_hbm,
    x, wq, wk, wv, q, k, v, rq, rk, in_sems, out_sems,
):
    loads = start_all((x_hbm, wq_hbm, wk_hbm, wv_hbm), (x, wq, wk, wv), in_sems)
    buffers = (q, rq, k, rk, v)
    outs = (q_hbm, rq_hbm, k_hbm, rk_hbm, v_hbm)
    stores = [
        pltpu.make_async_copy(buffer, out, out_sems.at[place])
        for place, (buffer, out) in enumerate(zip(buffers, outs))
    ]
    means = head_mean_matrix(256)
    loads[0].wait()
    rows = normed_rows(x, gain_ref)
    for weight, out, scale_out, factor, place in ((wq, q, rq, Q_SCALE, 0), (wk, k, rk, 1.0, 1)):
        loads[place + 1].wait()
        raw = dot(rows, weight[...])
        for index, scale in enumerate(head_scales(raw, means, 1e-06)):
            columns = slice(index * 256, index * 256 + 256)
            out[:, columns] = (raw[:, columns] * scale * factor).astype(BF16)
            scale_out[:, columns] = scale.astype(BF16)
        stores[2 * place].start()
        stores[2 * place + 1].start()
    loads[3].wait()
    v[...] = dot(rows, wv[...]).astype(BF16)
    stores[4].start()
    wait_all(stores)


def project(x, gain, wq, wk, wv):
    shape = pltpu.HBM((ROWS, WIDTH), BF16)
    square = pltpu.VMEM((WIDTH, WIDTH), BF16)
    rows = pltpu.VMEM((ROWS, WIDTH), BF16)
    return pl.pallas_call(
        project_kernel,
        in_specs=[HBM, WHOLE, HBM, HBM, HBM],
        out_specs=[HBM] * 5,
        out_shape=[shape] * 5,
        scratch_shapes=[
            rows, square, square, square, rows, rows, rows, rows, rows,
            pltpu.SemaphoreType.DMA((4,)),
            pltpu.SemaphoreType.DMA((5,)),
        ],
        compiler_params=params(56),
        name="project_own",
    )(x, gain, wq, wk, wv)


def live_points(cycle_points_ref, cycle):
    index = lax.axis_index(("chip", "core")) * (ROWS // CYCLE_MAX) - WINDOW // CYCLE_MAX + cycle
    count = cycle_points_ref.shape[0]
    points = cycle_points_ref[jnp.clip(index, 0, count - 1)]
    return jnp.where((index >= 0) & (index < count), points, 0)


def key_extras(points_ref):
    pieces = []
    lanes = lane((CYCLE_MAX, PAIR))
    slots = lax.broadcasted_iota(jnp.int32, (CYCLE_MAX, PAIR), 0)
    for cycle in range(EXT // CYCLE_MAX):
        bias = jnp.where(slots < live_points(points_ref, cycle), 0.0, DEAD)
        pieces.append(jnp.where(lanes == 0, bias, jnp.where(lanes < 3, 1.0, 0.0)).astype(BF16))
    return pieces


def by_head(value, low):
    zero = jnp.zeros_like(value)
    return jnp.concatenate([jnp.where(low, value, zero), jnp.where(low, zero, value)], 0)


def window_mask(shape, query_dim):
    queries = lax.broadcasted_iota(jnp.int32, shape, query_dim) & 255
    keys = lax.broadcasted_iota(jnp.int32, shape, 1 - query_dim)
    return (keys >= queries) & (keys <= queries + 2 * WINDOW)


def attend_pair(q, kx, vx, low, inside, one):
    lanes = lane((512, PAIR))
    spans = [slice(block * 256, block * 256 + 768) for block in range(2)]
    scores = []
    for block in range(2):
        left = jnp.concatenate([by_head(q[block * 256 : block * 256 + 256], low), one], 1)
        scores.append(dot_t(left, kx[spans[block]]))
    weights = [jnp.where(inside, jnp.exp2(score), 0.0).astype(BF16) for score in scores]
    rows, extras = [], []
    for block in range(2):
        total = dot(weights[block], vx[spans[block]])
        sums = total[:, PAIR:]
        out = total[:, :PAIR] / sums
        rows.append(jnp.where(low, out[:256], out[256:]).astype(BF16))
        shift = -jnp.log2(sums)
        high = shift.astype(BF16).astype(F32)
        extra = jnp.where(
            lanes == 0, 1.0, jnp.where(lanes == 1, high, jnp.where(lanes == 2, shift - high, 0.0))
        )
        extras.append(extra.astype(BF16))
    return rows, extras


def front_kernel(
    points_ref, before_hbm, after_hbm, wk_hbm, wv_hbm, q_hbm, k_hbm, v_hbm, x_hbm, wo_hbm,
    gain_ref, dec_gain_ref, wd_ref,
    kx_hbm, vx_hbm, att_hbm, eq_hbm, z_hbm, r_hbm, field_hbm, copies_hbm,
    halo, wk, wv, q, ke, ve, x, wo, att, eq, z, r, field, kx, vx, in_sems, out_sems,
):
    own = pl.ds(256, 512)
    loads = start_all(
        (before_hbm, after_hbm, wk_hbm, wv_hbm, q_hbm, k_hbm, v_hbm, wo_hbm, x_hbm),
        (halo.at[pl.ds(0, 256)], halo.at[pl.ds(256, 256)], wk, wv, q, ke.at[own], ve.at[own], wo, x),
        in_sems,
    )
    for cycle, piece in enumerate(key_extras(points_ref)):
        kx[cycle * CYCLE_MAX : (cycle + 1) * CYCLE_MAX, PAIR:] = piece
    vx[:, PAIR:] = jnp.ones((EXT, PAIR), BF16)
    means = head_mean_matrix(256)
    wait_all(loads[:3])
    rows = normed_rows(halo, gain_ref)
    raw = dot(rows, wk[...])
    for index, scale in enumerate(head_scales(raw, means, 1e-06)):
        columns = slice(index * 256, index * 256 + 256)
        part = (raw[:, columns] * scale).astype(BF16)
        ke[:256, columns] = part[:256]
        ke[768:, columns] = part[256:]
    loads[3].wait()
    part = dot(rows, wv[...]).astype(BF16)
    ve[:256] = part[:256]
    ve[768:] = part[256:]
    wait_all(loads[4:7])
    stores = start_all((ke, ve), (kx_hbm, vx_hbm), out_sems)
    low = lane((256, PAIR)) < HEAD_DIM
    one = jnp.where(lane((512, PAIR)) == 0, 1.0, 0.0).astype(BF16)
    inside = window_mask((512, 768), 0)

    def pair_step(pair, carry):
        columns = pl.ds(pl.multiple_of(pair * PAIR, PAIR), PAIR)
        kx[:, :PAIR] = ke[:, columns]
        vx[:, :PAIR] = ve[:, columns]
        rows, extras = attend_pair(q[:, columns], kx, vx, low, inside, one)
        for block in range(2):
            att[block * 256 : block * 256 + 256, columns] = rows[block]
            eq[pair, block * 512 : block * 512 + 512] = extras[block]
        return carry

    lax.fori_loop(0, PAIRS, pair_step, 0)
    stores += [
        pltpu.make_async_copy(source, target, out_sems.at[2 + place])
        for place, (source, target) in enumerate(
            ((att, att_hbm), (eq, eq_hbm), (z, z_hbm), (r, r_hbm), (field, field_hbm))
        )
    ]
    stores += [
        pltpu.make_async_copy(field, copies_hbm.at[member], out_sems.at[7 + member])
        for member in range(copies_hbm.shape[0])
    ]
    stores[2].start()
    stores[3].start()
    wait_all(loads[7:])
    level = x[...].astype(F32) + dot(att[...], wo[...])
    scale = lax.rsqrt(jnp.mean(level * level, -1, keepdims=True) + 1e-05)
    normal = level * scale
    decoded = (normal * dec_gain_ref[...]).astype(BF16)
    field[...] = dot_t(wd_ref[...], decoded).astype(BF16)
    for store in stores[6:]:
        store.start()
    z[...] = normal.astype(BF16)
    r[...] = jnp.broadcast_to(scale, r.shape)
    stores[4].start()
    stores[5].start()
    wait_all(stores)


def front(live, before, after, wk, wv, q, k, v, x, wo, gain, dec_gain, wd, members):
    variables = wd.shape[0]
    square = pltpu.VMEM((WIDTH, WIDTH), BF16)
    rows = pltpu.VMEM((ROWS, WIDTH), BF16)
    shape = pltpu.HBM((ROWS, WIDTH), BF16)
    ext = pltpu.HBM((EXT, WIDTH), BF16)
    return pl.pallas_call(
        front_kernel,
        in_specs=[pl.BlockSpec(memory_space=pltpu.SMEM)] + [HBM] * 9 + [WHOLE] * 3,
        out_specs=[HBM] * 8,
        out_shape=[
            ext,
            ext,
            shape,
            pltpu.HBM((PAIRS, EXT, PAIR), BF16),
            shape,
            pltpu.HBM((ROWS, PAIR), F32),
            pltpu.HBM((variables, ROWS), BF16),
            pltpu.HBM((members, variables, ROWS), BF16),
        ],
        scratch_shapes=[
            rows, square, square, rows,
            pltpu.VMEM((EXT, WIDTH), BF16),
            pltpu.VMEM((EXT, WIDTH), BF16),
            rows, square, rows,
            pltpu.VMEM((PAIRS, EXT, PAIR), BF16),
            rows,
            pltpu.VMEM((ROWS, PAIR), F32),
            pltpu.VMEM((variables, ROWS), BF16),
            pltpu.VMEM((EXT, 2 * PAIR), BF16),
            pltpu.VMEM((EXT, 2 * PAIR), BF16),
            pltpu.SemaphoreType.DMA((9,)),
            pltpu.SemaphoreType.DMA((7 + members,)),
        ],
        compiler_params=params(56),
        name="halo_attention_decode",
    )(live, before, after, wk, wv, q, k, v, x, wo, gain, dec_gain, wd)


def weights_kernel(points_ref, q_ref, ke_ref, eq_ref, edge_ref, own_ref, kx):
    @pl.when(pl.program_id(0) == 0)
    def _():
        for cycle, piece in enumerate(key_extras(points_ref)):
            kx[cycle * CYCLE_MAX : (cycle + 1) * CYCLE_MAX, PAIR:] = piece

    kx[:, :PAIR] = ke_ref[...]
    low = lane((256, PAIR)) < HEAD_DIM
    inside = window_mask((768, 512), 1)
    for block in range(2):
        q = by_head(q_ref[block * 256 : block * 256 + 256], low)
        left = jnp.concatenate([q, eq_ref[0, block * 512 : block * 512 + 512]], 1)
        scores = dot_t(kx[block * 256 : block * 256 + 768], left)
        weights = jnp.where(inside, jnp.exp2(scores), 0.0).astype(BF16)
        edge_ref[0, block] = weights[:256] if block == 0 else weights[512:]
        own_ref[0, block] = weights[256:] if block == 0 else weights[:512]


def attention_weights(live, q, ke, eq):
    part = pl.BlockSpec((ROWS, PAIR), lambda h, _: (0, h))
    ext = pl.BlockSpec((EXT, PAIR), lambda h, _: (0, h))
    return pl.pallas_call(
        weights_kernel,
        grid_spec=pltpu.PrefetchScalarGridSpec(
            num_scalar_prefetch=1,
            grid=(PAIRS,),
            in_specs=[part, ext, pl.BlockSpec((1, EXT, PAIR), lambda h, _: (h, 0, 0))],
            out_specs=[
                pl.BlockSpec((1, 2, 256, 512), lambda h, _: (h, 0, 0, 0)),
                pl.BlockSpec((1, 2, 512, 512), lambda h, _: (h, 0, 0, 0)),
            ],
            scratch_shapes=[pltpu.VMEM((EXT, 2 * PAIR), BF16)],
        ),
        out_shape=[
            pltpu.HBM((PAIRS, 2, 256, 512), BF16),
            pltpu.HBM((PAIRS, 2, 512, 512), BF16),
        ],
        compiler_params=params(56),
        cost_estimate=cost(8),
        name="attention_weights",
    )(live, q, ke, eq)


def slope_operands(q_rows, att_rows, da_rows, low):
    lanes = lane((512, PAIR))
    feature = lax.broadcasted_iota(jnp.int32, (PAIR, 2 * PAIR), 0) // HEAD_DIM
    column = lane((PAIR, 2 * PAIR))
    wanted = (feature == column // PAIR) & ((column % PAIR == 1) | (column % PAIR == 2))
    summing = jnp.where(wanted, 1.0, 0.0).astype(BF16)
    q = by_head(q_rows, low)
    da = by_head(da_rows, low)
    product = (da_rows.astype(F32) * att_rows.astype(F32)).astype(BF16)
    sums = dot(product, summing)
    sums = jnp.concatenate([sums[:, :PAIR], sums[:, PAIR:]], 0)
    top = sums.astype(BF16).astype(F32)
    offsets = jnp.where(lanes == 2, top - sums, -sums).astype(BF16)
    return q, da, jnp.concatenate([da, offsets], 1)


def ones_extra(count):
    lanes = lane((count, PAIR))
    return jnp.where((lanes == 1) | (lanes == 2), 1.0, 0.0).astype(BF16)


def query_piece(keys, slope):
    turned = keys.T
    halves = []
    for first in (0, 128):
        piece = jnp.concatenate(
            [
                dot(turned[:HEAD_DIM], slope[:, first : first + 128]),
                dot(turned[HEAD_DIM:], slope[:, first + 256 : first + 384]),
            ],
            0,
        )
        halves.append((piece * HEAD_DIM**-0.5).T)
    return jnp.concatenate(halves, 0)


def own_kernel(
    q_ref, ka_ref, kb_ref, va_ref, vb_ref, att_ref, da_ref, w_ref, part_ref, dq_ref, dk_ref, dv_ref
):
    low = lane((256, PAIR)) < HEAD_DIM
    values = jnp.concatenate([va_ref[...], vb_ref[...]], 0)
    values = jnp.concatenate([values, ones_extra(512)], 1)
    keys = jnp.concatenate([ka_ref[...], kb_ref[...]], 0)
    operands, slopes = [], []
    for block in range(2):
        rows = slice(block * 256, block * 256 + 256)
        operands.append(slope_operands(q_ref[rows], att_ref[rows], da_ref[rows], low))
        slope = w_ref[0, block].astype(F32) * dot_t(values, operands[block][2])
        slopes.append(slope.astype(BF16))
    weights = jnp.concatenate([w_ref[0, 0], w_ref[0, 1]], 1)
    dv_ref[...] = dot(weights, jnp.concatenate([operands[0][1], operands[1][1]], 0)).astype(BF16)
    dk = dot(jnp.concatenate(slopes, 1), jnp.concatenate([operands[0][0], operands[1][0]], 0))
    dk_ref[...] = (dk * (1.0 / LOG2E)).astype(BF16)
    for block in range(2):
        rows = slice(block * 256, block * 256 + 256)
        piece = query_piece(keys, slopes[block])
        dq_ref[rows] = (part_ref[rows].astype(F32) + piece).astype(BF16)


def own_backward(q, ke, ve, att, da, weights, dq):
    part = pl.BlockSpec((ROWS, PAIR), lambda h: (0, h))
    second = pl.BlockSpec((256, PAIR), lambda h: (1, h))
    third = pl.BlockSpec((256, PAIR), lambda h: (2, h))
    shape = pltpu.HBM((ROWS, WIDTH), BF16)
    return pl.pallas_call(
        own_kernel,
        grid=(PAIRS,),
        in_specs=[part, second, third, second, third, part, part]
        + [pl.BlockSpec((1, 2, 512, 512), lambda h: (h, 0, 0, 0)), part],
        out_specs=[part] * 3,
        out_shape=[shape] * 3,
        compiler_params=params(56),
        cost_estimate=cost(15),
        name="own_backward",
    )(q, ke, ke, ve, ve, att, da, weights, dq)


def kernel_slope(diff):
    return diff * lax.rsqrt(diff * diff + 0.01)


def score_kernel(
    points_ref, own_ref, all_hbm, target_hbm, z_hbm, r_hbm, gain_ref, wd_ref, wo_hbm, att_hbm,
    q_hbm, ke_hbm, ve_hbm, w_hbm,
    lg_hbm, da_hbm, mine_hbm, theirs_hbm, dq_hbm, low_hbm, high_hbm,
    everyone, target, z, r, wo, att, q, ke, ve, w, lg, da, term, dq, edges,
    in_sems, edge_sems, out_sems,
):
    halves = (pl.ds(0, 256), pl.ds(768, 256))
    loads = start_all(
        [all_hbm, target_hbm, z_hbm, r_hbm, att_hbm, wo_hbm, q_hbm]
        + [ref.at[half] for ref in (ve_hbm, ke_hbm) for half in halves]
        + [w_hbm],
        [everyone, target, z, r, att, wo, q]
        + [ref.at[half] for ref in (ve, ke) for half in range(2)]
        + [w],
        in_sems,
    )
    stores = [
        pltpu.make_async_copy(source, place, out_sems.at[index])
        for index, (source, place) in enumerate(
            (
                (lg, lg_hbm),
                (da, da_hbm),
                (term.at[lax.axis_index("core")], mine_hbm),
                (term.at[1 - lax.axis_index("core")], theirs_hbm),
                (dq, dq_hbm),
            )
        )
    ]
    members = everyone.shape[0]
    own = own_ref[...].astype(F32)
    slots = lane((own.shape[0], CYCLE_MAX))
    live = jnp.concatenate(
        [jnp.where(slots < live_points(points_ref, 2 + cycle), 1.0, 0.0) for cycle in range(ROWS // CYCLE_MAX)], 1
    )
    wait_all(loads[:2])
    pair_sum = None
    for member in range(members):
        slope = kernel_slope(own - everyone[member].astype(F32))
        pair_sum = slope if pair_sum is None else pair_sum + slope
    grad = (kernel_slope(own - target[...]) - pair_sum * (1.0 / (members - 1))) * live
    back = lax.dot_general(
        grad.astype(BF16), wd_ref[...], (((0,), (0,)), ((), ())), preferred_element_type=F32
    )
    back = back.astype(BF16).astype(F32) * gain_ref[...]
    wait_all(loads[2:4])
    normal = z[...].astype(F32)
    level_grad = r[:, :1] * (back - normal * jnp.mean(back * normal, -1, keepdims=True))
    lg[...] = level_grad.astype(BF16)
    stores[0].start()
    wait_all(loads[4:6])
    da[...] = dot_t(lg[...], wo[...]).astype(BF16)
    stores[1].start()
    whole = lax.dot_general(
        att[...], lg[...], (((0,), (0,)), ((), ())), preferred_element_type=F32
    ).astype(BF16)
    for row in range(16):
        for column in range(8):
            for half in range(2):
                first = row * 64 + half * 32
                term[half, row, column] = whole[
                    first : first + 32, column * 128 : column * 128 + 128
                ]
    stores[2].start()
    stores[3].start()
    wait_all(loads[6:])

    low = lane((256, PAIR)) < HEAD_DIM
    ones = ones_extra(256)

    def store(pair, block):
        columns = pl.ds(pl.multiple_of(pair * PAIR, PAIR), PAIR)
        place = (low_hbm, high_hbm)[block]
        return pltpu.make_async_copy(
            edges.at[block, :, :, columns], place.at[:, :, columns], edge_sems.at[block, pair]
        )

    def pair_step(step, carry):
        for pair in [step * 4 + place for place in range(4)]:
            columns = pl.ds(pl.multiple_of(pair * PAIR, PAIR), PAIR)
            for block in range(2):
                rows = slice(block * 256, block * 256 + 256)
                queries, grads, left = slope_operands(
                    q[rows, columns], att[rows, columns], da[rows, columns], low
                )
                weights = w[pair, block]
                slope = dot_t(jnp.concatenate([ve[block, :, columns], ones], 1), left)
                slope = (weights.astype(F32) * slope).astype(BF16)
                edges[block, 0, :, columns] = (dot(slope, queries) * (1.0 / LOG2E)).astype(BF16)
                edges[block, 1, :, columns] = dot(weights, grads).astype(BF16)
                dq[rows, columns] = query_piece(ke[block, :, columns], slope).astype(BF16)
        for pair in [step * 4 + place for place in range(4)]:
            for block in range(2):
                store(pair, block).start()
        return carry

    lax.fori_loop(0, PAIRS // 4, pair_step, 0)
    stores[4].start()
    for pair in range(PAIRS):
        for block in range(2):
            store(pair, block).wait()
    wait_all(stores)


def score(live, own, everyone, target, z, r, gain, wd, wo, att, q, ke, ve, weights):
    square = pltpu.VMEM((WIDTH, WIDTH), BF16)
    rows = pltpu.VMEM((ROWS, WIDTH), BF16)
    halves = pltpu.VMEM((2, 256, WIDTH), BF16)
    shape = pltpu.HBM((ROWS, WIDTH), BF16)
    edge = pltpu.HBM((2, 256, WIDTH), BF16)
    term = pltpu.HBM((16, 8, 32, 128), BF16)
    return pl.pallas_call(
        score_kernel,
        in_specs=[pl.BlockSpec(memory_space=pltpu.SMEM), WHOLE]
        + [HBM] * 4 + [WHOLE] * 2 + [HBM] * 6,
        out_specs=[HBM] * 7,
        out_shape=[shape, shape, term, term, shape, edge, edge],
        scratch_shapes=[
            pltpu.VMEM(everyone.shape, BF16),
            pltpu.VMEM(target.shape, F32),
            rows,
            pltpu.VMEM((ROWS, PAIR), F32),
            square, rows, rows, halves, halves,
            pltpu.VMEM((PAIRS, 2, 256, 512), BF16),
            rows, rows,
            pltpu.VMEM((2, 16, 8, 32, 128), BF16),
            rows,
            pltpu.VMEM((2, 2, 256, WIDTH), BF16),
            pltpu.SemaphoreType.DMA((12,)),
            pltpu.SemaphoreType.DMA((2, PAIRS)),
            pltpu.SemaphoreType.DMA((5,)),
        ],
        compiler_params=params(50),
        cost_estimate=cost(15),
        name="score_and_edges",
    )(live, own, everyone, target, z, r, gain, wd, wo, att, q, ke, ve, weights)


def final_kernel(
    x_hbm, gain_ref, q_hbm, rq_hbm, dq_hbm, wq_hbm, dv_hbm, before_hbm, after_hbm, wv_hbm,
    dk_hbm, k_hbm, rk_hbm, wk_hbm, lg_hbm, out_hbm,
    x, q, rq, dq, wq, dv, before, after, wv, dk, k, rk, wk, lg, out, in_sems, out_sems,
):
    loads = start_all(
        (q_hbm, rq_hbm, dq_hbm, wq_hbm, dv_hbm, before_hbm, after_hbm, wv_hbm,
         dk_hbm, k_hbm, rk_hbm, wk_hbm, x_hbm, lg_hbm),
        (q, rq, dq, wq, dv, before, after, wv, dk, k, rk, wk, x, lg),
        in_sems,
    )
    means = head_mean_matrix(256)

    def norm_back(y, scale, grad):
        product = (y * grad).astype(BF16)
        mean = jnp.concatenate(
            [dot(product[:, c : c + 256], means) for c in range(0, WIDTH, 256)], 1
        )
        return (scale.astype(F32) * (grad - y * mean)).astype(BF16)

    def gathered(own, kind):
        halo = jnp.concatenate([before[kind], after[kind]], 0)
        return own[...].astype(F32) + halo.astype(F32)

    wait_all(loads[:3])
    q_in = norm_back(q[...].astype(F32) * (1.0 / Q_SCALE), rq[...], dq[...].astype(F32))
    loads[3].wait()
    total = dot_t(q_in, wq[...])
    wait_all(loads[4:8])
    total += dot_t(gathered(dv, 1).astype(BF16), wv[...])
    wait_all(loads[8:12])
    k_in = norm_back(k[...].astype(F32), rk[...], gathered(dk, 0))
    total += dot_t(k_in, wk[...])
    wait_all(loads[12:])
    stores = []
    for block in range(2):
        rows = slice(block * 256, block * 256 + 256)
        state = x[rows].astype(F32)
        scale = lax.rsqrt(jnp.mean(state * state, -1, keepdims=True) + 1e-05)
        grad = total[rows] * gain_ref[...]
        y = state * scale
        back = scale * (grad - y * jnp.mean(grad * y, -1, keepdims=True))
        out[rows] = lg[rows].astype(F32) + back
        place = pl.ds(block * 256, 256)
        stores.append(pltpu.make_async_copy(out.at[place], out_hbm.at[place], out_sems.at[block]))
        stores[-1].start()
    wait_all(stores)


def finish(x, gain, q, k, rq, rk, dq, dk, dv, before, after, wq, wk, wv, lg):
    square = pltpu.VMEM((WIDTH, WIDTH), BF16)
    rows = pltpu.VMEM((ROWS, WIDTH), BF16)
    edge = pltpu.VMEM((2, 256, WIDTH), BF16)
    return pl.pallas_call(
        final_kernel,
        in_specs=[HBM, WHOLE] + [HBM] * 13,
        out_specs=HBM,
        out_shape=pltpu.HBM((ROWS, WIDTH), F32),
        scratch_shapes=[
            rows, rows, rows, rows, square, rows, edge, edge, square, rows, rows, rows, square, rows,
            pltpu.VMEM((ROWS, WIDTH), F32),
            pltpu.SemaphoreType.DMA((14,)),
            pltpu.SemaphoreType.DMA((2,)),
        ],
        compiler_params=params(53),
        name="finish",
    )(x, gain, q, rq, dq, wq, dv, before, after, wv, dk, k, rk, wk, lg)


def body(
    latent_grids, cycle_points, norm_gain, w_query, w_key, w_value, w_out, dec_gain, w_dec, target
):
    x = latent_grids[0]
    grid = ("chip", "core")
    bands = lax.axis_size(grid)
    up = [(i, i + 1) for i in range(bands - 1)]
    down = [(j, i) for i, j in up]
    norm_gain = norm_gain[None]
    dec_gain = dec_gain[None]

    before = lax.ppermute(x[256:], grid, up)
    after = lax.ppermute(x[:256], grid, down)
    q, k, v, rq, rk = project(x, norm_gain, w_query, w_key, w_value)
    members = lax.axis_size("member")
    ke, ve, att, eq, z, r, field, copies = front(
        cycle_points, before, after, w_key, w_value, q, k, v, x, w_out, norm_gain, dec_gain, w_dec, members
    )
    everyone = lax.all_to_all(copies, "member", 0, 0, tiled=True)
    edge_weights, own_weights = attention_weights(cycle_points, q, ke, eq)
    lg, da, mine, theirs, dq, low, high = score(
        cycle_points, field, everyone, target, z, r, dec_gain, w_dec, w_out, att, q, ke, ve, edge_weights
    )
    sibling = lax.ppermute(theirs, "core", [(0, 1), (1, 0)])
    grad_before = lax.ppermute(high, grid, up)
    grad_after = lax.ppermute(low, grid, down)
    dq, dk, dv = own_backward(q, ke, ve, att, da, own_weights, dq)
    sens = finish(
        x, norm_gain, q, k, rq, rk, dq, dk, dv, grad_before, grad_after,
        w_query, w_key, w_value, lg,
    )
    blocks = (mine.astype(F32) + sibling.astype(F32)).astype(BF16)
    pieces = lax.all_to_all(
        blocks.reshape(128, 32, 128), ("chip", "core", "member"), 0, 0, tiled=True
    )
    halves = jnp.sum(pieces.reshape(8, 2, 8, 32, 128).astype(F32), (0, 2))
    out = halves.reshape(64, 128)
    return (field[None], sens[None], out)


def solution(mesh):
    members, bands = mesh.devices.shape
    mesh = Mesh(mesh.devices.reshape(members, bands // 2, 2), ("member", "chip", "core"))
    grid = ("chip", "core")
    placed = (P("member", grid, None), P(), P(), P(), P(), P(), P(), P(), P(), P(None, grid))
    return jax.shard_map(
        body,
        mesh=mesh,
        in_specs=placed,
        out_specs=(P("member", None, grid), P("member", grid, None), P(grid, "member")),
        check_vma=False,
    )
```

```python
import jax
import jax.numpy as jnp
from jax import lax
from jax.experimental import pallas as pl
from jax.experimental.pallas import tpu as pltpu
from jax.sharding import Mesh, PartitionSpec as P

HEAD_DIM = 64
CYCLE_MAX = 128
WINDOW = 256
ROWS = 512
EXT = 1024
WIDTH = 1024
PAIR = 128
PAIRS = 8
LOG2E = 1.4426950408889634
Q_SCALE = LOG2E * HEAD_DIM**-0.5
DEAD = -30000.0
F32 = jnp.float32
BF16 = jnp.bfloat16


def params(mib):
    return pltpu.CompilerParams(vmem_limit_bytes=mib * 1024 * 1024)


def cost(gigaflops):
    return pl.CostEstimate(flops=int(gigaflops * 1e9), bytes_accessed=4 << 20, transcendentals=0)


def dot(left, right):
    return lax.dot_general(left, right, (((1,), (0,)), ((), ())), preferred_element_type=F32)


def dot_t(left, right):
    return lax.dot_general(left, right, (((1,), (1,)), ((), ())), preferred_element_type=F32)


def lane(shape):
    return lax.broadcasted_iota(jnp.int32, shape, len(shape) - 1)


def head_mean_matrix(width):
    rows = lax.broadcasted_iota(jnp.int32, (width, width), 0) // HEAD_DIM
    cols = lax.broadcasted_iota(jnp.int32, (width, width), 1) // HEAD_DIM
    return jnp.where(rows == cols, 1.0 / HEAD_DIM, 0.0).astype(BF16)


def normed_rows(x_ref, gain_ref):
    x = x_ref[...].astype(F32)
    scale = lax.rsqrt(jnp.mean(x * x, -1, keepdims=True) + 1e-05)
    return (x * scale * gain_ref[...]).astype(BF16)


HBM = pl.BlockSpec(memory_space=pl.ANY)
WHOLE = pl.BlockSpec(memory_space=pltpu.VMEM)


def start_all(sources, targets, semaphores):
    copies = [
        pltpu.make_async_copy(source, target, semaphores.at[place])
        for place, (source, target) in enumerate(zip(sources, targets))
    ]
    for copy in copies:
        copy.start()
    return copies


def wait_all(copies):
    for copy in copies:
        copy.wait()


def head_scales(raw, means, epsilon):
    return [
        lax.rsqrt(dot((part * part).astype(BF16), means) + epsilon)
        for part in (raw[:, c : c + 256] for c in range(0, WIDTH, 256))
    ]


def project_kernel(
    x_hbm, gain_ref, wq_hbm, wk_hbm, wv_hbm, q_hbm, k_hbm, v_hbm, rq_hbm, rk_hbm,
    x, wq, wk, wv, q, k, v, rq, rk, in_sems, out_sems,
):
    loads = start_all((x_hbm, wq_hbm, wk_hbm, wv_hbm), (x, wq, wk, wv), in_sems)
    buffers = (q, rq, k, rk, v)
    outs = (q_hbm, rq_hbm, k_hbm, rk_hbm, v_hbm)
    stores = [
        pltpu.make_async_copy(buffer, out, out_sems.at[place])
        for place, (buffer, out) in enumerate(zip(buffers, outs))
    ]
    means = head_mean_matrix(256)
    loads[0].wait()
    rows = normed_rows(x, gain_ref)
    for weight, out, scale_out, factor, place in ((wq, q, rq, Q_SCALE, 0), (wk, k, rk, 1.0, 1)):
        loads[place + 1].wait()
        raw = dot(rows, weight[...])
        for index, scale in enumerate(head_scales(raw, means, 1e-06)):
            columns = slice(index * 256, index * 256 + 256)
            out[:, columns] = (raw[:, columns] * scale * factor).astype(BF16)
            scale_out[:, columns] = scale.astype(BF16)
        stores[2 * place].start()
        stores[2 * place + 1].start()
    loads[3].wait()
    v[...] = dot(rows, wv[...]).astype(BF16)
    stores[4].start()
    wait_all(stores)


def project(x, gain, wq, wk, wv):
    shape = pltpu.HBM((ROWS, WIDTH), BF16)
    square = pltpu.VMEM((WIDTH, WIDTH), BF16)
    rows = pltpu.VMEM((ROWS, WIDTH), BF16)
    return pl.pallas_call(
        project_kernel,
        in_specs=[HBM, WHOLE, HBM, HBM, HBM],
        out_specs=[HBM] * 5,
        out_shape=[shape] * 5,
        scratch_shapes=[
            rows, square, square, square, rows, rows, rows, rows, rows,
            pltpu.SemaphoreType.DMA((4,)),
            pltpu.SemaphoreType.DMA((5,)),
        ],
        compiler_params=params(56),
        name="project_own",
    )(x, gain, wq, wk, wv)


def live_points(cycle_points_ref, cycle):
    index = lax.axis_index(("chip", "core")) * (ROWS // CYCLE_MAX) - WINDOW // CYCLE_MAX + cycle
    count = cycle_points_ref.shape[0]
    points = cycle_points_ref[jnp.clip(index, 0, count - 1)]
    return jnp.where((index >= 0) & (index < count), points, 0)


def key_extras(points_ref):
    pieces = []
    lanes = lane((CYCLE_MAX, PAIR))
    slots = lax.broadcasted_iota(jnp.int32, (CYCLE_MAX, PAIR), 0)
    for cycle in range(EXT // CYCLE_MAX):
        bias = jnp.where(slots < live_points(points_ref, cycle), 0.0, DEAD)
        pieces.append(jnp.where(lanes == 0, bias, jnp.where(lanes < 3, 1.0, 0.0)).astype(BF16))
    return pieces


def by_head(value, low):
    zero = jnp.zeros_like(value)
    return jnp.concatenate([jnp.where(low, value, zero), jnp.where(low, zero, value)], 0)


def window_mask(shape, query_dim):
    queries = lax.broadcasted_iota(jnp.int32, shape, query_dim) & 255
    keys = lax.broadcasted_iota(jnp.int32, shape, 1 - query_dim)
    return (keys >= queries) & (keys <= queries + 2 * WINDOW)


def attend_pair(q, kx, vx, low, inside, one):
    lanes = lane((512, PAIR))
    spans = [slice(block * 256, block * 256 + 768) for block in range(2)]
    scores = []
    for block in range(2):
        left = jnp.concatenate([by_head(q[block * 256 : block * 256 + 256], low), one], 1)
        scores.append(dot_t(left, kx[spans[block]]))
    weights = [jnp.where(inside, jnp.exp2(score), 0.0).astype(BF16) for score in scores]
    rows, extras = [], []
    for block in range(2):
        total = dot(weights[block], vx[spans[block]])
        sums = total[:, PAIR:]
        out = total[:, :PAIR] / sums
        rows.append(jnp.where(low, out[:256], out[256:]).astype(BF16))
        shift = -jnp.log2(sums)
        high = shift.astype(BF16).astype(F32)
        extra = jnp.where(
            lanes == 0, 1.0, jnp.where(lanes == 1, high, jnp.where(lanes == 2, shift - high, 0.0))
        )
        extras.append(extra.astype(BF16))
    return rows, extras


def front_kernel(
    points_ref, before_hbm, after_hbm, wk_hbm, wv_hbm, q_hbm, k_hbm, v_hbm, x_hbm, wo_hbm,
    gain_ref, dec_gain_ref, wd_ref,
    kx_hbm, vx_hbm, att_hbm, eq_hbm, z_hbm, r_hbm, field_hbm, copies_hbm,
    halo, wk, wv, q, ke, ve, x, wo, att, eq, z, r, field, kx, vx, in_sems, out_sems,
):
    own = pl.ds(256, 512)
    loads = start_all(
        (before_hbm, after_hbm, wk_hbm, wv_hbm, q_hbm, k_hbm, v_hbm, wo_hbm, x_hbm),
        (halo.at[pl.ds(0, 256)], halo.at[pl.ds(256, 256)], wk, wv, q, ke.at[own], ve.at[own], wo, x),
        in_sems,
    )
    for cycle, piece in enumerate(key_extras(points_ref)):
        kx[cycle * CYCLE_MAX : (cycle + 1) * CYCLE_MAX, PAIR:] = piece
    vx[:, PAIR:] = jnp.ones((EXT, PAIR), BF16)
    means = head_mean_matrix(256)
    wait_all(loads[:3])
    rows = normed_rows(halo, gain_ref)
    raw = dot(rows, wk[...])
    for index, scale in enumerate(head_scales(raw, means, 1e-06)):
        columns = slice(index * 256, index * 256 + 256)
        part = (raw[:, columns] * scale).astype(BF16)
        ke[:256, columns] = part[:256]
        ke[768:, columns] = part[256:]
    loads[3].wait()
    part = dot(rows, wv[...]).astype(BF16)
    ve[:256] = part[:256]
    ve[768:] = part[256:]
    wait_all(loads[4:7])
    stores = start_all((ke, ve), (kx_hbm, vx_hbm), out_sems)
    low = lane((256, PAIR)) < HEAD_DIM
    one = jnp.where(lane((512, PAIR)) == 0, 1.0, 0.0).astype(BF16)
    inside = window_mask((512, 768), 0)

    def pair_step(pair, carry):
        columns = pl.ds(pl.multiple_of(pair * PAIR, PAIR), PAIR)
        kx[:, :PAIR] = ke[:, columns]
        vx[:, :PAIR] = ve[:, columns]
        rows, extras = attend_pair(q[:, columns], kx, vx, low, inside, one)
        for block in range(2):
            att[block * 256 : block * 256 + 256, columns] = rows[block]
            eq[pair, block * 512 : block * 512 + 512] = extras[block]
        return carry

    lax.fori_loop(0, PAIRS, pair_step, 0)
    stores += [
        pltpu.make_async_copy(source, target, out_sems.at[2 + place])
        for place, (source, target) in enumerate(
            ((att, att_hbm), (eq, eq_hbm), (z, z_hbm), (r, r_hbm), (field, field_hbm))
        )
    ]
    stores += [
        pltpu.make_async_copy(field, copies_hbm.at[member], out_sems.at[7 + member])
        for member in range(copies_hbm.shape[0])
    ]
    stores[2].start()
    stores[3].start()
    wait_all(loads[7:])
    level = x[...].astype(F32) + dot(att[...], wo[...])
    scale = lax.rsqrt(jnp.mean(level * level, -1, keepdims=True) + 1e-05)
    normal = level * scale
    decoded = (normal * dec_gain_ref[...]).astype(BF16)
    field[...] = dot_t(wd_ref[...], decoded).astype(BF16)
    for store in stores[6:]:
        store.start()
    z[...] = normal.astype(BF16)
    r[...] = jnp.broadcast_to(scale, r.shape)
    stores[4].start()
    stores[5].start()
    wait_all(stores)


def front(live, before, after, wk, wv, q, k, v, x, wo, gain, dec_gain, wd, members):
    variables = wd.shape[0]
    square = pltpu.VMEM((WIDTH, WIDTH), BF16)
    rows = pltpu.VMEM((ROWS, WIDTH), BF16)
    shape = pltpu.HBM((ROWS, WIDTH), BF16)
    ext = pltpu.HBM((EXT, WIDTH), BF16)
    return pl.pallas_call(
        front_kernel,
        in_specs=[pl.BlockSpec(memory_space=pltpu.SMEM)] + [HBM] * 9 + [WHOLE] * 3,
        out_specs=[HBM] * 8,
        out_shape=[
            ext,
            ext,
            shape,
            pltpu.HBM((PAIRS, EXT, PAIR), BF16),
            shape,
            pltpu.HBM((ROWS, PAIR), F32),
            pltpu.HBM((variables, ROWS), BF16),
            pltpu.HBM((members, variables, ROWS), BF16),
        ],
        scratch_shapes=[
            rows, square, square, rows,
            pltpu.VMEM((EXT, WIDTH), BF16),
            pltpu.VMEM((EXT, WIDTH), BF16),
            rows, square, rows,
            pltpu.VMEM((PAIRS, EXT, PAIR), BF16),
            rows,
            pltpu.VMEM((ROWS, PAIR), F32),
            pltpu.VMEM((variables, ROWS), BF16),
            pltpu.VMEM((EXT, 2 * PAIR), BF16),
            pltpu.VMEM((EXT, 2 * PAIR), BF16),
            pltpu.SemaphoreType.DMA((9,)),
            pltpu.SemaphoreType.DMA((7 + members,)),
        ],
        compiler_params=params(56),
        name="halo_attention_decode",
    )(live, before, after, wk, wv, q, k, v, x, wo, gain, dec_gain, wd)


def weights_kernel(points_ref, q_ref, ke_ref, eq_ref, edge_ref, own_ref, kx):
    @pl.when(pl.program_id(0) == 0)
    def _():
        for cycle, piece in enumerate(key_extras(points_ref)):
            kx[cycle * CYCLE_MAX : (cycle + 1) * CYCLE_MAX, PAIR:] = piece

    kx[:, :PAIR] = ke_ref[...]
    low = lane((256, PAIR)) < HEAD_DIM
    inside = window_mask((768, 512), 1)
    for block in range(2):
        q = by_head(q_ref[block * 256 : block * 256 + 256], low)
        left = jnp.concatenate([q, eq_ref[0, block * 512 : block * 512 + 512]], 1)
        scores = dot_t(kx[block * 256 : block * 256 + 768], left)
        weights = jnp.where(inside, jnp.exp2(scores), 0.0).astype(BF16)
        edge_ref[0, block] = weights[:256] if block == 0 else weights[512:]
        own_ref[0, block] = weights[256:] if block == 0 else weights[:512]


def attention_weights(live, q, ke, eq):
    part = pl.BlockSpec((ROWS, PAIR), lambda h, _: (0, h))
    ext = pl.BlockSpec((EXT, PAIR), lambda h, _: (0, h))
    return pl.pallas_call(
        weights_kernel,
        grid_spec=pltpu.PrefetchScalarGridSpec(
            num_scalar_prefetch=1,
            grid=(PAIRS,),
            in_specs=[part, ext, pl.BlockSpec((1, EXT, PAIR), lambda h, _: (h, 0, 0))],
            out_specs=[
                pl.BlockSpec((1, 2, 256, 512), lambda h, _: (h, 0, 0, 0)),
                pl.BlockSpec((1, 2, 512, 512), lambda h, _: (h, 0, 0, 0)),
            ],
            scratch_shapes=[pltpu.VMEM((EXT, 2 * PAIR), BF16)],
        ),
        out_shape=[
            pltpu.HBM((PAIRS, 2, 256, 512), BF16),
            pltpu.HBM((PAIRS, 2, 512, 512), BF16),
        ],
        compiler_params=params(56),
        cost_estimate=cost(8),
        name="attention_weights",
    )(live, q, ke, eq)


def slope_operands(q_rows, att_rows, da_rows, low):
    lanes = lane((512, PAIR))
    feature = lax.broadcasted_iota(jnp.int32, (PAIR, 2 * PAIR), 0) // HEAD_DIM
    column = lane((PAIR, 2 * PAIR))
    wanted = (feature == column // PAIR) & ((column % PAIR == 1) | (column % PAIR == 2))
    summing = jnp.where(wanted, 1.0, 0.0).astype(BF16)
    q = by_head(q_rows, low)
    da = by_head(da_rows, low)
    product = (da_rows.astype(F32) * att_rows.astype(F32)).astype(BF16)
    sums = dot(product, summing)
    sums = jnp.concatenate([sums[:, :PAIR], sums[:, PAIR:]], 0)
    top = sums.astype(BF16).astype(F32)
    offsets = jnp.where(lanes == 2, top - sums, -sums).astype(BF16)
    return q, da, jnp.concatenate([da, offsets], 1)


def ones_extra(count):
    lanes = lane((count, PAIR))
    return jnp.where((lanes == 1) | (lanes == 2), 1.0, 0.0).astype(BF16)


def query_piece(keys, slope):
    turned = keys.T
    halves = []
    for first in (0, 128):
        piece = jnp.concatenate(
            [
                dot(turned[:HEAD_DIM], slope[:, first : first + 128]),
                dot(turned[HEAD_DIM:], slope[:, first + 256 : first + 384]),
            ],
            0,
        )
        halves.append((piece * HEAD_DIM**-0.5).T)
    return jnp.concatenate(halves, 0)


def own_pair(
    q_ref, ka_ref, kb_ref, va_ref, vb_ref, att_ref, da_ref, w_ref, part_ref, dq_ref, dk_ref, dv_ref, side
):
    low = lane((256, PAIR)) < HEAD_DIM
    values = jnp.concatenate([va_ref[...], vb_ref[...]], 0)
    values = jnp.concatenate([values, ones_extra(512)], 1)
    keys = jnp.concatenate([ka_ref[...], kb_ref[...]], 0)
    operands, slopes = [], []
    for block in range(2):
        rows = slice(block * 256, block * 256 + 256)
        operands.append(slope_operands(q_ref[rows], att_ref[rows], da_ref[rows], low))
        slope = w_ref[side, block].astype(F32) * dot_t(values, operands[block][2])
        slopes.append(slope.astype(BF16))
    weights = jnp.concatenate([w_ref[side, 0], w_ref[side, 1]], 1)
    dv_ref[...] = dot(weights, jnp.concatenate([operands[0][1], operands[1][1]], 0)).astype(BF16)
    dk = dot(jnp.concatenate(slopes, 1), jnp.concatenate([operands[0][0], operands[1][0]], 0))
    dk_ref[...] = (dk * (1.0 / LOG2E)).astype(BF16)
    for block in range(2):
        rows = slice(block * 256, block * 256 + 256)
        piece = query_piece(keys, slopes[block])
        dq_ref[rows] = (part_ref[rows].astype(F32) + piece).astype(BF16)


def own_kernel(*refs):
    for side in range(2):
        columns = slice(side * PAIR, side * PAIR + PAIR)
        own_pair(*(ref if place == 7 else ref.at[:, columns] for place, ref in enumerate(refs)), side)


def own_backward(q, ke, ve, att, da, weights, dq):
    part = pl.BlockSpec((ROWS, 2 * PAIR), lambda h: (0, h))
    second = pl.BlockSpec((256, 2 * PAIR), lambda h: (1, h))
    third = pl.BlockSpec((256, 2 * PAIR), lambda h: (2, h))
    shape = pltpu.HBM((ROWS, WIDTH), BF16)
    return pl.pallas_call(
        own_kernel,
        grid=(PAIRS // 2,),
        in_specs=[part, second, third, second, third, part, part]
        + [pl.BlockSpec((2, 2, 512, 512), lambda h: (h, 0, 0, 0)), part],
        out_specs=[part] * 3,
        out_shape=[shape] * 3,
        compiler_params=params(56),
        cost_estimate=cost(15),
        name="own_backward",
    )(q, ke, ke, ve, ve, att, da, weights, dq)


def kernel_slope(diff):
    return diff * lax.rsqrt(diff * diff + 0.01)


def score_kernel(
    points_ref, own_ref, all_hbm, target_hbm, z_hbm, r_hbm, gain_ref, wd_ref, wo_hbm, att_hbm,
    q_hbm, ke_hbm, ve_hbm, w_hbm,
    lg_hbm, da_hbm, mine_hbm, theirs_hbm, dq_hbm, low_hbm, high_hbm,
    everyone, target, z, r, wo, att, q, ke, ve, w, lg, da, term, dq, edges,
    in_sems, edge_sems, out_sems,
):
    halves = (pl.ds(0, 256), pl.ds(768, 256))
    loads = start_all(
        [all_hbm, target_hbm, z_hbm, r_hbm, att_hbm, wo_hbm, q_hbm]
        + [ref.at[half] for ref in (ve_hbm, ke_hbm) for half in halves]
        + [w_hbm],
        [everyone, target, z, r, att, wo, q]
        + [ref.at[half] for ref in (ve, ke) for half in range(2)]
        + [w],
        in_sems,
    )
    stores = [
        pltpu.make_async_copy(source, place, out_sems.at[index])
        for index, (source, place) in enumerate(
            (
                (lg, lg_hbm),
                (da, da_hbm),
                (term.at[lax.axis_index("core")], mine_hbm),
                (term.at[1 - lax.axis_index("core")], theirs_hbm),
                (dq, dq_hbm),
            )
        )
    ]
    members = everyone.shape[0]
    own = own_ref[...].astype(F32)
    slots = lane((own.shape[0], CYCLE_MAX))
    live = jnp.concatenate(
        [jnp.where(slots < live_points(points_ref, 2 + cycle), 1.0, 0.0) for cycle in range(ROWS // CYCLE_MAX)], 1
    )
    wait_all(loads[:2])
    pair_sum = None
    for member in range(members):
        slope = kernel_slope(own - everyone[member].astype(F32))
        pair_sum = slope if pair_sum is None else pair_sum + slope
    grad = (kernel_slope(own - target[...]) - pair_sum * (1.0 / (members - 1))) * live
    back = lax.dot_general(
        grad.astype(BF16), wd_ref[...], (((0,), (0,)), ((), ())), preferred_element_type=F32
    )
    back = back.astype(BF16).astype(F32) * gain_ref[...]
    wait_all(loads[2:4])
    normal = z[...].astype(F32)
    level_grad = r[:, :1] * (back - normal * jnp.mean(back * normal, -1, keepdims=True))
    lg[...] = level_grad.astype(BF16)
    stores[0].start()
    wait_all(loads[4:6])
    da[...] = dot_t(lg[...], wo[...]).astype(BF16)
    stores[1].start()
    whole = lax.dot_general(
        att[...], lg[...], (((0,), (0,)), ((), ())), preferred_element_type=F32
    ).astype(BF16)
    for row in range(16):
        for column in range(8):
            for half in range(2):
                first = row * 64 + half * 32
                term[half, row, column] = whole[
                    first : first + 32, column * 128 : column * 128 + 128
                ]
    stores[2].start()
    stores[3].start()
    wait_all(loads[6:])

    low = lane((256, PAIR)) < HEAD_DIM
    ones = ones_extra(256)

    def store(pair, block):
        columns = pl.ds(pl.multiple_of(pair * PAIR, PAIR), PAIR)
        place = (low_hbm, high_hbm)[block]
        return pltpu.make_async_copy(
            edges.at[block, :, :, columns], place.at[:, :, columns], edge_sems.at[block, pair]
        )

    def pair_step(step, carry):
        for pair in [step * 4 + place for place in range(4)]:
            columns = pl.ds(pl.multiple_of(pair * PAIR, PAIR), PAIR)
            for block in range(2):
                rows = slice(block * 256, block * 256 + 256)
                queries, grads, left = slope_operands(
                    q[rows, columns], att[rows, columns], da[rows, columns], low
                )
                weights = w[pair, block]
                slope = dot_t(jnp.concatenate([ve[block, :, columns], ones], 1), left)
                slope = (weights.astype(F32) * slope).astype(BF16)
                edges[block, 0, :, columns] = (dot(slope, queries) * (1.0 / LOG2E)).astype(BF16)
                edges[block, 1, :, columns] = dot(weights, grads).astype(BF16)
                dq[rows, columns] = query_piece(ke[block, :, columns], slope).astype(BF16)
        for pair in [step * 4 + place for place in range(4)]:
            for block in range(2):
                store(pair, block).start()
        return carry

    lax.fori_loop(0, PAIRS // 4, pair_step, 0)
    stores[4].start()
    for pair in range(PAIRS):
        for block in range(2):
            store(pair, block).wait()
    wait_all(stores)


def score(live, own, everyone, target, z, r, gain, wd, wo, att, q, ke, ve, weights):
    square = pltpu.VMEM((WIDTH, WIDTH), BF16)
    rows = pltpu.VMEM((ROWS, WIDTH), BF16)
    halves = pltpu.VMEM((2, 256, WIDTH), BF16)
    shape = pltpu.HBM((ROWS, WIDTH), BF16)
    edge = pltpu.HBM((2, 256, WIDTH), BF16)
    term = pltpu.HBM((16, 8, 32, 128), BF16)
    return pl.pallas_call(
        score_kernel,
        in_specs=[pl.BlockSpec(memory_space=pltpu.SMEM), WHOLE]
        + [HBM] * 4 + [WHOLE] * 2 + [HBM] * 6,
        out_specs=[HBM] * 7,
        out_shape=[shape, shape, term, term, shape, edge, edge],
        scratch_shapes=[
            pltpu.VMEM(everyone.shape, BF16),
            pltpu.VMEM(target.shape, F32),
            rows,
            pltpu.VMEM((ROWS, PAIR), F32),
            square, rows, rows, halves, halves,
            pltpu.VMEM((PAIRS, 2, 256, 512), BF16),
            rows, rows,
            pltpu.VMEM((2, 16, 8, 32, 128), BF16),
            rows,
            pltpu.VMEM((2, 2, 256, WIDTH), BF16),
            pltpu.SemaphoreType.DMA((12,)),
            pltpu.SemaphoreType.DMA((2, PAIRS)),
            pltpu.SemaphoreType.DMA((5,)),
        ],
        compiler_params=params(50),
        cost_estimate=cost(15),
        name="score_and_edges",
    )(live, own, everyone, target, z, r, gain, wd, wo, att, q, ke, ve, weights)


def final_kernel(
    x_hbm, gain_ref, q_hbm, rq_hbm, dq_hbm, wq_hbm, dv_hbm, before_hbm, after_hbm, wv_hbm,
    dk_hbm, k_hbm, rk_hbm, wk_hbm, lg_hbm, out_hbm,
    x, q, rq, dq, wq, dv, before, after, wv, dk, k, rk, wk, lg, out, in_sems, out_sems,
):
    loads = start_all(
        (q_hbm, rq_hbm, dq_hbm, wq_hbm, dv_hbm, before_hbm, after_hbm, wv_hbm,
         dk_hbm, k_hbm, rk_hbm, wk_hbm, x_hbm, lg_hbm),
        (q, rq, dq, wq, dv, before, after, wv, dk, k, rk, wk, x, lg),
        in_sems,
    )
    means = head_mean_matrix(256)

    def norm_back(y, scale, grad):
        product = (y * grad).astype(BF16)
        mean = jnp.concatenate(
            [dot(product[:, c : c + 256], means) for c in range(0, WIDTH, 256)], 1
        )
        return (scale.astype(F32) * (grad - y * mean)).astype(BF16)

    def gathered(own, kind):
        halo = jnp.concatenate([before[kind], after[kind]], 0)
        return own[...].astype(F32) + halo.astype(F32)

    wait_all(loads[:3])
    q_in = norm_back(q[...].astype(F32) * (1.0 / Q_SCALE), rq[...], dq[...].astype(F32))
    loads[3].wait()
    total = dot_t(q_in, wq[...])
    wait_all(loads[4:8])
    total += dot_t(gathered(dv, 1).astype(BF16), wv[...])
    wait_all(loads[8:12])
    k_in = norm_back(k[...].astype(F32), rk[...], gathered(dk, 0))
    total += dot_t(k_in, wk[...])
    wait_all(loads[12:])
    stores = []
    for block in range(2):
        rows = slice(block * 256, block * 256 + 256)
        state = x[rows].astype(F32)
        scale = lax.rsqrt(jnp.mean(state * state, -1, keepdims=True) + 1e-05)
        grad = total[rows] * gain_ref[...]
        y = state * scale
        back = scale * (grad - y * jnp.mean(grad * y, -1, keepdims=True))
        out[rows] = lg[rows].astype(F32) + back
        place = pl.ds(block * 256, 256)
        stores.append(pltpu.make_async_copy(out.at[place], out_hbm.at[place], out_sems.at[block]))
        stores[-1].start()
    wait_all(stores)


def finish(x, gain, q, k, rq, rk, dq, dk, dv, before, after, wq, wk, wv, lg):
    square = pltpu.VMEM((WIDTH, WIDTH), BF16)
    rows = pltpu.VMEM((ROWS, WIDTH), BF16)
    edge = pltpu.VMEM((2, 256, WIDTH), BF16)
    return pl.pallas_call(
        final_kernel,
        in_specs=[HBM, WHOLE] + [HBM] * 13,
        out_specs=HBM,
        out_shape=pltpu.HBM((ROWS, WIDTH), F32),
        scratch_shapes=[
            rows, rows, rows, rows, square, rows, edge, edge, square, rows, rows, rows, square, rows,
            pltpu.VMEM((ROWS, WIDTH), F32),
            pltpu.SemaphoreType.DMA((14,)),
            pltpu.SemaphoreType.DMA((2,)),
        ],
        compiler_params=params(53),
        name="finish",
    )(x, gain, q, rq, dq, wq, dv, before, after, wv, dk, k, rk, wk, lg)


def body(
    latent_grids, cycle_points, norm_gain, w_query, w_key, w_value, w_out, dec_gain, w_dec, target
):
    x = latent_grids[0]
    grid = ("chip", "core")
    bands = lax.axis_size(grid)
    up = [(i, i + 1) for i in range(bands - 1)]
    down = [(j, i) for i, j in up]
    norm_gain = norm_gain[None]
    dec_gain = dec_gain[None]

    before = lax.ppermute(x[256:], grid, up)
    after = lax.ppermute(x[:256], grid, down)
    q, k, v, rq, rk = project(x, norm_gain, w_query, w_key, w_value)
    members = lax.axis_size("member")
    ke, ve, att, eq, z, r, field, copies = front(
        cycle_points, before, after, w_key, w_value, q, k, v, x, w_out, norm_gain, dec_gain, w_dec, members
    )
    everyone = lax.all_to_all(copies, "member", 0, 0, tiled=True)
    edge_weights, own_weights = attention_weights(cycle_points, q, ke, eq)
    lg, da, mine, theirs, dq, low, high = score(
        cycle_points, field, everyone, target, z, r, dec_gain, w_dec, w_out, att, q, ke, ve, edge_weights
    )
    sibling = lax.ppermute(theirs, "core", [(0, 1), (1, 0)])
    grad_before = lax.ppermute(high, grid, up)
    grad_after = lax.ppermute(low, grid, down)
    dq, dk, dv = own_backward(q, ke, ve, att, da, own_weights, dq)
    sens = finish(
        x, norm_gain, q, k, rq, rk, dq, dk, dv, grad_before, grad_after,
        w_query, w_key, w_value, lg,
    )
    blocks = (mine.astype(F32) + sibling.astype(F32)).astype(BF16)
    pieces = lax.all_to_all(
        blocks.reshape(128, 32, 128), ("chip", "core", "member"), 0, 0, tiled=True
    )
    halves = jnp.sum(pieces.reshape(8, 2, 8, 32, 128).astype(F32), (0, 2))
    out = halves.reshape(64, 128)
    return (field[None], sens[None], out)


def solution(mesh):
    members, bands = mesh.devices.shape
    mesh = Mesh(mesh.devices.reshape(members, bands // 2, 2), ("member", "chip", "core"))
    grid = ("chip", "core")
    placed = (P("member", grid, None), P(), P(), P(), P(), P(), P(), P(), P(), P(None, grid))
    return jax.shard_map(
        body,
        mesh=mesh,
        in_specs=placed,
        out_specs=(P("member", None, grid), P("member", grid, None), P(grid, "member")),
        check_vma=False,
    )
```
